32 devices in a mesh: row: 4 (over x, core), col: 8 (over z, y).
Axes of the slice: x: 2, y: 2, z: 4, core: 2. Of those that a mesh axis runs over, the one named last changes fastest.
Arguments:
- pair: float32 [512, 512, 128], P('row', 'col'), may hold values from -6 to 6
- logit_cotangent: bfloat16 [512, 512, 64], P('row', 'col'), may hold values from -6 to 6
- tiles: bfloat16 [512, 1024, 64], P(('row', 'col')), may hold values from -6 to 6
- tile_target: int32 [512, 1], P(('row', 'col')), may hold values from 0 to 7; in each aligned block of 16 rows (0 to 15, 16 to 31, ...) at most 2 rows name the same one
- tile_square: int32 [512], P(('row', 'col')), may hold values from 0 to 7
- tile_count: int32 [512], P(('row', 'col')), may hold values from 1 to 4
- w_template: bfloat16 [64, 128], replicated, may hold values from -0.75 to 0.75
- transition_norm_gain: float32 [128], replicated, may hold values from 0.1 to 1.9
- transition_norm_bias: float32 [128], replicated, may hold values from -3 to 3
- w_gate: bfloat16 [128, 512], replicated, may hold values from -0.5 to 0.5
- w_up: bfloat16 [128, 512], replicated, may hold values from -0.5 to 0.5
- w_out: bfloat16 [512, 128], replicated, may hold values from -0.25 to 0.25
- w_dist: bfloat16 [128, 64], replicated, may hold values from -0.5 to 0.5
Outputs:
- logits: bfloat16 [512, 512, 64], P('row', 'col')
- grad_pair: float32 [512, 512, 128], P('row', 'col')
- grad_tiles: bfloat16 [512, 1024, 64], P(('row', 'col'))
- grad_template: float32 [64, 128], replicated
- grad_gain: float32 [128], replicated
- grad_bias: float32 [128], replicated
- grad_gate: float32 [128, 512], replicated
- grad_up: float32 [128, 512], replicated
- grad_out: float32 [512, 128], replicated
- grad_dist: float32 [128, 64], replicated
The draws below stay inside these ranges and needn't reach their ends.
Inputs may be any that keep to these rules, and one draw needn't show every extreme that they name: `tile_target`: among the 16 tiles of one device no column device is named more than 2 times; some device names one exactly 2 times.
All inputs are finite; a program needn't handle non-finite values.
Results may differ from the reference program's by a relative error of at most 0.0079.
Values may be sent and summed in bfloat16 or wider, within the bound.
No kernel may reach another device: no remote copies, remote signals or barrier semaphores. Data moves between devices by JAX's collectives and lax.ppermute only.
A program may use at most 128 MiB of HBM per device.

```python
import math
import jax
import jax.numpy as jnp
import numpy as np
from jax import lax

C = 128
TW = 64
HID = 512
BINS = 64
SQ = 32
SLOTS = 16
CAP = 2
ROW_DEV = 128
CROP = 512
COL_DEV = 64
SQ_DEV = 8
TILES = 512
N_ROW = 4
N_COL = 8


def set_ends(result, key, least, largest):
    longest = result.shape.index(max(result.shape))
    spots = []
    for shift in (0, 1):
        where = [jax.random.randint(jax.random.fold_in(key, axis), (), 0, length) for axis, length in enumerate(result.shape)]
        where[longest] = (where[longest] + shift) % result.shape[longest]
        spots.append(tuple(where))
    return result.at[spots[0]].set(least).at[spots[1]].set(largest)


def steps_of(own_key, shape, shards, smallest, top_value):
    factor_of, own = 1.0, jax.random.fold_in(own_key, 6)
    for position, parts in shards:
        steps = jnp.exp(jax.random.uniform(jax.random.fold_in(own, position), (parts,), jnp.float32, smallest / len(shards), top_value / len(shards)))
        factor_of = factor_of * jnp.repeat(steps, shape[position] // parts).reshape([-1 if axis == position else 1 for axis in range(len(shape))])
    return factor_of


def deal_out(key, own, number, rows, amount, top, most, lean):
    order = jax.random.permutation(key, amount)
    packed, ordinary = shares(amount, rows * top, most, lean, True), shares(amount, rows * top, most, lean, False)
    places = jnp.arange(amount)

    def named(lengths, turn):
        used = int((lengths > 0).sum())
        fixed = max(1, used // 4)
        passed = fixed + (places - fixed + turn * (used - fixed)) % max(1, amount - fixed)
        return jnp.zeros((amount,), jnp.int32).at[order[jnp.where(places < fixed, places, passed)]].set(jnp.asarray(lengths, jnp.int32))

    lengths = jnp.where(number % 4 == 0, named(packed, number // 4), named(ordinary, number - number // 4 - 1))
    mixed = jax.random.permutation(jax.random.fold_in(own, 3), amount)
    giver, receiver = mixed[0:amount // 2 * 2:2], mixed[1:amount // 2 * 2:2]
    margin = jnp.minimum(lengths[giver] - 1, most - lengths[receiver]) // 2
    margin = jnp.where((giver == order[0]) | (receiver == order[0]) | (lengths[receiver] == 0), 0, jnp.maximum(margin, 0))
    passed = jax.random.randint(jax.random.fold_in(own, 4), (amount // 2,), 0, 1 << 20) % (margin + 1)
    lengths = lengths.at[giver].add(-passed).at[receiver].add(passed)
    members = jnp.searchsorted(jnp.cumsum(lengths), jnp.arange(rows * top), side="right").astype(jnp.int32)
    table = members.reshape(top, rows).T
    table = table[jax.random.permutation(jax.random.fold_in(own, 1), rows)]
    turn = jax.random.randint(jax.random.fold_in(own, 2), (rows, 1), 0, top)
    return jnp.take_along_axis(table, (jnp.arange(top)[None, :] + turn) % top, axis=1)


def shares(amount, total, most, lean, full):
    weights = [(1 << 20) // math.isqrt(standing ** lean) + 1 for standing in range(1, amount + 1)]
    largest = most if full else min(most, max(-(-total // amount), total * weights[0] // sum(weights)))
    least = 1 if total - largest >= amount - 1 else 0
    holding, surplus = [largest] + [least] * (amount - 1), total - largest - least * (amount - 1)
    while surplus > 0:
        free = [i for i in range(1, amount) if holding[i] < largest] or [i for i in range(1, amount) if holding[i] < most]
        mass, left = sum([weights[i] for i in free]), surplus
        for i in free:
            addition = min(most - holding[i], max(1, left * weights[i] // mass), surplus)
            holding[i] = holding[i] + addition
            surplus = surplus - addition
    return np.array(holding)


def normal_values(rng, dims, deviation, bound, split=(), kind=jnp.bfloat16):
    level = steps_of(rng, dims, split, -0.22, 0.18) if split else 1.0
    entries = jax.random.normal(rng, dims, jnp.float32) * deviation * level
    return jnp.minimum(jnp.maximum(entries, -bound), bound).astype(kind)


def setup_inputs(seed: int = 0) -> dict:
    splits = jax.random.split(jax.random.key(seed), 14)
    pair = normal_values(splits[0], (CROP, CROP, C), 1.0, 6.0, ((0, 4), (1, 8)), jnp.float32)
    logit_cotangent = normal_values(splits[1], (CROP, CROP, BINS), 1.0, 6.0, ((0, 4), (1, 8)))
    tiles = normal_values(splits[2], (TILES, SQ * SQ, TW), 1.0, 6.0, ((0, 32),))
    tile_target_keys = jax.random.split(jax.random.fold_in(splits[3], 1), TILES // SLOTS)
    tile_target_turns = jax.random.permutation(jax.random.fold_in(splits[3], 3), TILES // SLOTS)
    tile_target = jax.vmap(lambda own, number: deal_out(jax.random.fold_in(splits[3], 2), own, number, SLOTS, N_COL, 1, CAP, 2))(tile_target_keys, tile_target_turns).reshape((TILES, 1))
    tile_square = set_ends(jax.random.randint(splits[4], (TILES,), 0, SQ_DEV), jax.random.fold_in(splits[4], 1), 0, SQ_DEV - 1).astype(jnp.int32)
    tile_count = set_ends(jax.random.randint(splits[5], (TILES,), 1, 5), jax.random.fold_in(splits[5], 1), 1, 4).astype(jnp.int32)
    w_template = normal_values(splits[6], (TW, C), TW ** -0.5, 0.75)
    transition_norm_gain = jnp.clip(1.0 + 0.18 * jax.random.normal(splits[7], (C,), jnp.float32), 0.1, 1.9)
    transition_norm_bias = normal_values(splits[8], (C,), 0.5, 3.0, (), jnp.float32)
    w_gate = normal_values(splits[9], (C, HID), C ** -0.5, 0.5)
    w_up = normal_values(splits[10], (C, HID), C ** -0.5, 0.5)
    w_out = normal_values(splits[11], (HID, C), HID ** -0.5, 0.25)
    w_dist = normal_values(splits[12], (C, BINS), C ** -0.5, 0.5)
    return {"pair": pair, "logit_cotangent": logit_cotangent, "tiles": tiles, "tile_target": tile_target, "tile_square": tile_square, "tile_count": tile_count, "w_template": w_template, "transition_norm_gain": transition_norm_gain, "transition_norm_bias": transition_norm_bias, "w_gate": w_gate, "w_up": w_up, "w_out": w_out, "w_dist": w_dist}


def squares_to_grid(values, across, downward):
    return values.reshape(across, downward, SQ, SQ, -1).transpose(0, 2, 1, 3, 4).reshape(across * SQ, downward * SQ, -1)

def grid_to_squares(values, across, downward):
    return values.reshape(across, SQ, downward, SQ, -1).transpose(0, 2, 1, 3, 4).reshape(across * downward, SQ * SQ, -1)

def norm_intermediates(pair_entries, transition_norm_gain, transition_norm_bias):
    centered_entries = pair_entries - lax.optimization_barrier(jnp.mean(pair_entries, axis=-1, keepdims=True))
    inverse_deviation = lax.rsqrt(lax.optimization_barrier(jnp.mean(centered_entries * centered_entries, axis=-1, keepdims=True)) + 1e-05)
    standardized_entries = centered_entries * inverse_deviation
    return (standardized_entries, inverse_deviation, (standardized_entries * transition_norm_gain + transition_norm_bias).astype(jnp.bfloat16))

def transition_forward(pair_entries, transition_norm_gain, transition_norm_bias, w_gate, w_up, w_out):
    standardized_entries, inverse_deviation, normalized_entries = norm_intermediates(pair_entries, transition_norm_gain, transition_norm_bias)
    gate = jnp.dot(normalized_entries, w_gate, preferred_element_type=jnp.float32)
    upper = jnp.dot(normalized_entries, w_up, preferred_element_type=jnp.float32)
    hidden = (jax.nn.silu(gate) * upper).astype(jnp.bfloat16)
    return pair_entries + jnp.dot(hidden, w_out, preferred_element_type=jnp.float32)

def transition_backward(pair_entries, upstream, transition_norm_gain, transition_norm_bias, w_gate, w_up, w_out):
    standardized_entries, inverse_deviation, normalized_entries = norm_intermediates(pair_entries, transition_norm_gain, transition_norm_bias)
    gate = jnp.dot(normalized_entries, w_gate, preferred_element_type=jnp.float32)
    upper = jnp.dot(normalized_entries, w_up, preferred_element_type=jnp.float32)
    sigma = jax.nn.sigmoid(gate)
    swish = gate * sigma
    hidden = (swish * upper).astype(jnp.bfloat16)
    up_low = upstream.astype(jnp.bfloat16)
    g_out = jnp.dot(hidden.T, up_low, preferred_element_type=jnp.float32)
    d_hidden = jnp.dot(up_low, w_out.T, preferred_element_type=jnp.float32)
    d_gate = (d_hidden * upper * sigma * (1.0 + gate * (1.0 - sigma))).astype(jnp.bfloat16)
    d_upper = (d_hidden * swish).astype(jnp.bfloat16)
    g_gate = jnp.dot(normalized_entries.T, d_gate, preferred_element_type=jnp.float32)
    g_up = jnp.dot(normalized_entries.T, d_upper, preferred_element_type=jnp.float32)
    normalized_gradient = jnp.dot(d_gate, w_gate.T, preferred_element_type=jnp.float32) + jnp.dot(d_upper, w_up.T, preferred_element_type=jnp.float32)
    gain_gradient = lax.optimization_barrier(jnp.sum(normalized_gradient * standardized_entries, axis=0))
    g_bias = lax.optimization_barrier(jnp.sum(normalized_gradient, axis=0))
    standardized_gradient = normalized_gradient * transition_norm_gain
    entries_gradient = (standardized_gradient - lax.optimization_barrier(jnp.mean(standardized_gradient, axis=-1, keepdims=True)) - standardized_entries * lax.optimization_barrier(jnp.mean(standardized_gradient * standardized_entries, axis=-1, keepdims=True))) * inverse_deviation
    return (upstream + entries_gradient, (gain_gradient, g_bias, g_gate, g_up, g_out))

def reference(pair, logit_cotangent, tiles, tile_target, tile_square, tile_count, w_template, transition_norm_gain, transition_norm_bias, w_gate, w_up, w_out, w_dist):
    length = ROW_DEV * N_ROW
    side = length // SQ
    per_row = COL_DEV // SQ
    cells_sq = SQ * SQ
    target = tile_target[:, 0].astype(jnp.int32)
    holder = jnp.arange(TILES, dtype=jnp.int32) // SLOTS
    owner_row = holder // N_COL
    square_row = owner_row * (ROW_DEV // SQ) + tile_square // per_row
    square_col = target * per_row + tile_square % per_row
    global_ids = (square_row * side + square_col).astype(jnp.int32)
    counts_f = tile_count.astype(jnp.float32)
    group = SLOTS * 8
    groups = TILES // group
    tiles_g = tiles.reshape(groups, group, cells_sq, TW)
    ids_g = global_ids.reshape(groups, group)
    counts_g = counts_f.reshape(groups, group)

    def add_group(totals, items):
        piece, ident, weight = items
        proj = jnp.dot(piece.reshape(group * cells_sq, TW), w_template, preferred_element_type=jnp.float32)
        proj = (proj.reshape(group, cells_sq, C) / weight[:, None, None]).astype(jnp.bfloat16).astype(jnp.float32)
        return (totals.at[ident].add(proj), None)
    totals, unused = lax.scan(add_group, jnp.zeros((side * side, cells_sq, C), jnp.float32), (tiles_g, ids_g, counts_g))
    z_one = pair + squares_to_grid(totals, side, side)
    band = 8
    bands = length // band
    z_blocks = z_one.reshape(bands, band * length, C)
    z_two = lax.map(lambda piece: transition_forward(piece, transition_norm_gain, transition_norm_bias, w_gate, w_up, w_out), z_blocks)
    z_low = z_two.reshape(length * length, C).astype(jnp.bfloat16)
    heads = jnp.dot(z_low, w_dist, preferred_element_type=jnp.float32).astype(jnp.bfloat16).reshape(length, length, BINS)
    logits = (heads.astype(jnp.float32) + jnp.swapaxes(heads, 0, 1).astype(jnp.float32)).astype(jnp.bfloat16)
    d_heads = (logit_cotangent.astype(jnp.float32) + jnp.swapaxes(logit_cotangent, 0, 1).astype(jnp.float32)).astype(jnp.bfloat16)
    d_heads = d_heads.reshape(length * length, BINS)
    dz_two = jnp.dot(d_heads, w_dist.T, preferred_element_type=jnp.float32)
    g_dist = jnp.dot(z_low.T, d_heads, preferred_element_type=jnp.float32)

    def back_band(carry, items):
        piece, upstream = items
        d_piece, grads = transition_backward(piece, upstream, transition_norm_gain, transition_norm_bias, w_gate, w_up, w_out)
        return (tuple((total + term for total, term in zip(carry, grads))), d_piece)
    start = (jnp.zeros((C,), jnp.float32), jnp.zeros((C,), jnp.float32), jnp.zeros((C, HID), jnp.float32), jnp.zeros((C, HID), jnp.float32), jnp.zeros((HID, C), jnp.float32))
    sums, dz_one = lax.scan(back_band, start, (z_blocks, dz_two.reshape(bands, band * length, C)))
    grad_pair = dz_one.reshape(length, length, C)
    d_squares = grid_to_squares(grad_pair, side, side)

    def tile_back(carry, items):
        piece, ident, weight = items
        d_proj = d_squares[ident].astype(jnp.bfloat16)
        g_tile = jnp.dot(d_proj.reshape(group * cells_sq, C), w_template.T, preferred_element_type=jnp.float32)
        g_tile = (g_tile.reshape(group, cells_sq, TW) / weight[:, None, None]).astype(jnp.bfloat16)
        per_slot = jnp.einsum('spt,spc->stc', piece.astype(jnp.float32), d_proj.astype(jnp.float32))
        return (carry + lax.optimization_barrier(jnp.sum(per_slot / weight[:, None, None], axis=0)), g_tile)
    g_template, grad_tiles = lax.scan(tile_back, jnp.zeros((TW, C), jnp.float32), (tiles_g, ids_g, counts_g))
    grad_tiles = grad_tiles.reshape(TILES, cells_sq, TW)
    scale = jnp.float32(length)
    return (logits, grad_pair, grad_tiles, g_template / scale, sums[0] / scale, sums[1] / scale, sums[2] / scale, sums[3] / scale, sums[4] / scale, g_dist / scale)
```

```python
import functools

import jax
import jax.numpy as jnp
from jax import lax
from jax.experimental import pallas as pl
from jax.experimental.pallas import tpu as pltpu
from jax.sharding import PartitionSpec as P

SQ = 32
CAP = 2
LANES = 128
META = 16
GROUP = LANES // SQ
STEP_ROWS = 16
PIECE = 256
VMEM_BYTES = 52 * 2**20
BF16 = jnp.bfloat16
F32 = jnp.float32

VMEM = pl.BlockSpec(memory_space=pltpu.VMEM)
SMEM = pl.BlockSpec(memory_space=pltpu.SMEM)
ANY = pl.BlockSpec(memory_space=pl.ANY)


def params():
    return pltpu.CompilerParams(vmem_limit_bytes=VMEM_BYTES)


def dot_nn(a, b):
    return lax.dot_general(a, b, (((1,), (0,)), ((), ())), preferred_element_type=F32)


def dot_nt(a, b):
    return lax.dot_general(a, b, (((1,), (1,)), ((), ())), preferred_element_type=F32)


def dot_tn(a, b):
    return lax.dot_general(a, b, (((0,), (0,)), ((), ())), preferred_element_type=F32)


def fill_slots(me, target, source, devs):
    def clear(i, unused):
        source[i] = -1
        return unused

    def place(s, unused):
        place_of = lax.rem(target[s] - me + devs, devs) * CAP
        taken = source[place_of] >= 0
        source[place_of + jnp.where(taken, 1, 0)] = s
        return unused

    lax.fori_loop(0, devs * CAP, clear, 0)
    lax.fori_loop(0, target.shape[0], place, 0)


def low_lanes(shape):
    return lax.broadcasted_iota(jnp.int32, shape, 1) < LANES // 2


def pack_kernel(devs, where_am, target, square, count, tiles, cot, *refs):
    payloads, (cot_a, cot_b), (source,) = refs[:devs], refs[devs : devs + 2], refs[devs + 2 :]
    feature, cells = tiles.shape[1:]
    groups = cells // LANES
    fill_slots(where_am[0], target, source, devs)
    first = where_am[1] == 0
    low = low_lanes(cot.shape[1:])

    def pack_pair(p, unused):
        even, odd = cot[2 * p].astype(F32), cot[2 * p + 1].astype(F32)
        front = jnp.where(low, even, pltpu.roll(odd, LANES // 2, 1)).astype(BF16)
        back = jnp.where(low, pltpu.roll(even, LANES // 2, 1), odd).astype(BF16)
        cot_a[p] = jnp.where(first, front, back)
        cot_b[p] = jnp.where(first, back, front)
        return unused

    lax.fori_loop(0, cot.shape[0] // 2, pack_pair, 0, unroll=4)
    line = lax.broadcasted_iota(jnp.int32, (META, LANES), 0)
    for k in range(devs):
        meta = jnp.zeros((META, LANES), F32)
        for r in range(CAP):
            slot = source[k * CAP + r]
            held = jnp.maximum(slot, 0)
            ident = jnp.where(slot >= 0, square[held], -1).astype(F32)
            meta = jnp.where(line == r, ident, meta)
            meta = jnp.where(line == 8 + r, count[held].astype(F32), meta)
            for c in range(groups):
                at = (r * groups + c) * feature
                payloads[k][at : at + feature, :] = tiles[held, :, c * LANES : (c + 1) * LANES]
        payloads[k][CAP * groups * feature :, :] = meta.astype(BF16)


def cotangent_kernel(where_am, cot, got_a, got_b, out, turned):
    cols, bins, rows = cot.shape

    def turn(j, unused):
        turned[pl.ds(j, rows, stride=cols), 0:bins] = cot[j].astype(F32).T
        return unused

    lax.fori_loop(0, cols, turn, 0, unroll=4)
    pairs = got_a.shape[0]
    for half in range(rows // cols):
        straight = where_am[1] == half

        def add(p, unused):
            mirrored = jnp.where(straight, got_a[p].astype(F32), got_b[p].astype(F32)).T
            at = pl.multiple_of((half * pairs + p) * LANES, LANES)
            out[pl.ds(at, LANES), :] = (turned[pl.ds(at, LANES), 0:bins] + mirrored).astype(BF16)
            return unused

        lax.fori_loop(0, pairs, add, 0, unroll=4)


def fold_rows(values):
    return jnp.sum(values.reshape(values.shape[0] // 8, 8, values.shape[1]), axis=0)


def main_kernel(devs, cols, *refs):
    where_am, refs = refs[0], refs[1:]
    payloads, refs = refs[:devs], refs[devs:]
    (pair, dheads, w_template, gain, bias, w_gate, w_up, w_out, w_gate_t, w_up_t, w_out_t, w_dist_t), refs = refs[:12], refs[12:]
    (grad_pair, z_low_out, heads_a, heads_b), refs = refs[:4], refs[4:]
    returns, refs = refs[:devs], refs[devs:]
    (keep, send), refs = refs[:2], refs[2:]
    idents, total, summed, squares, acc_gu, acc_out, acc_td, acc_gb, low_gu, low_hid, sems = refs
    step = pl.program_id(0)
    steps = pl.num_programs(0)
    feature, width = w_template.shape
    hidden = w_gate.shape[1]
    groups = SQ * SQ // LANES
    slab = groups * feature
    block = pair.shape[0]
    rows = block // cols
    sq_cols = cols // SQ
    parts = SQ // rows
    per_part = groups // parts

    @pl.when(step == 0)
    def _():
        total[...] = jnp.zeros_like(total)
        acc_gu[...] = jnp.zeros_like(acc_gu)
        acc_out[...] = jnp.zeros_like(acc_out)
        acc_td[...] = jnp.zeros_like(acc_td)
        acc_gb[...] = jnp.zeros_like(acc_gb)
        for k in range(devs):
            meta = payloads[k][CAP * slab :, :].astype(F32)
            for r in range(CAP):
                ident = jnp.max(meta[r : r + 1, :]).astype(jnp.int32)
                idents[k * CAP + r] = ident
                scale = 1.0 / meta[8 + r : 9 + r, :]

                @pl.when(ident >= 0)
                def _():
                    at = pl.multiple_of(ident * slab, slab)
                    total[pl.ds(at, slab), :] += payloads[k][r * slab : (r + 1) * slab, :].astype(F32) * scale

        summed[...] = total[...].astype(BF16)

    band, part = step // parts, lax.rem(step, parts)
    proj, pieces = [], []
    for c in range(per_part):
        across = []
        for s in range(sq_cols):
            at = pl.multiple_of(((band * sq_cols + s) * groups + part * per_part + c) * feature, feature)
            piece = summed[pl.ds(at, feature), :]
            across.append(dot_tn(piece, w_template[...]).reshape(GROUP, SQ, width))
            pieces.append(piece)
        proj.append(jnp.concatenate(across, axis=1).reshape(GROUP * cols, width))
    z_one = pair[...] + jnp.concatenate(proj, axis=0)
    mean = jnp.mean(z_one, axis=1, keepdims=True)
    centred = z_one - mean
    deviation = lax.rsqrt(jnp.mean(centred * centred, axis=1, keepdims=True) + 1e-5)
    standard = centred * deviation
    normed = (standard * gain[...] + bias[...]).astype(BF16)
    d_low = dheads[...]
    dz_two = dot_nn(d_low, w_dist_t[...])
    dz_low = dz_two.astype(BF16)

    z_two = z_one
    d_norm = jnp.zeros_like(z_one)
    for h in range(0, hidden, PIECE):
        e = h + PIECE
        gate = dot_nn(normed, w_gate[:, h:e])
        upper = dot_nn(normed, w_up[:, h:e])
        d_hidden = dot_nn(dz_low, w_out_t[:, h:e])
        sigma = 0.5 * jnp.tanh(0.5 * gate) + 0.5
        swish = gate * sigma
        hid = (swish * upper).astype(BF16)
        d_gate = (d_hidden * upper * (sigma + swish * (1.0 - sigma))).astype(BF16)
        d_upper = (d_hidden * swish).astype(BF16)
        z_two = z_two + dot_nn(hid, w_out[h:e, :])
        d_norm = d_norm + dot_nn(d_gate, w_gate_t[h:e, :]) + dot_nn(d_upper, w_up_t[h:e, :])
        low_hid[:, h:e] = hid
        low_gu[:, h:e] = d_gate
        low_gu[:, hidden + h : hidden + e] = d_upper

    acc_gu[...] += dot_tn(normed, low_gu[...])
    acc_out[...] += dot_tn(dz_low, low_hid[...])
    z_low = z_two.astype(BF16)
    z_low_out[...] = z_low
    acc_td[feature:, :] += dot_tn(d_low, z_low)
    acc_gb[0:8, :] += fold_rows(d_norm * standard)
    acc_gb[8:16, :] += fold_rows(d_norm)
    d_standard = d_norm * gain[...]
    grad = dz_two + deviation * (
        d_standard
        - jnp.mean(d_standard, axis=1, keepdims=True)
        - standard * jnp.mean(d_standard * standard, axis=1, keepdims=True)
    )
    grad_pair[...] = grad

    heads = dot_nt(w_dist_t[...], z_low).astype(BF16)
    per_half = steps // 2
    pairs = block // LANES
    at = lax.rem(step, per_half) * pairs
    straight = step // per_half == where_am[1]

    @pl.when(straight)
    def _():
        for p in range(pairs):
            heads_a[at + p] = heads[:, p * LANES : (p + 1) * LANES]

    @pl.when(jnp.logical_not(straight))
    def _():
        for p in range(pairs):
            heads_b[at + p] = heads[:, p * LANES : (p + 1) * LANES]

    d_proj = grad.astype(BF16).reshape(rows, cols, width)
    for s in range(sq_cols):
        cells = d_proj[:, s * SQ : (s + 1) * SQ, :].reshape(rows * SQ, width)
        tile_grad = dot_nt(w_template[...], cells).astype(BF16)
        for c in range(per_part):
            at = pl.multiple_of((part * per_part + c) * feature, feature)
            squares[band * sq_cols + s, pl.ds(at, feature), :] = tile_grad[:, c * LANES : (c + 1) * LANES]
        side = jnp.concatenate([pieces[c * sq_cols + s] for c in range(per_part)], axis=1)
        acc_td[0:feature, :] += dot_nn(side, cells)

    @pl.when(step == steps - 1)
    def _():
        def copy_of(k, r):
            return pltpu.make_async_copy(
                squares.at[jnp.maximum(idents[k * CAP + r], 0)],
                returns[k].at[pl.ds(r * slab, slab)],
                sems.at[k * CAP + r],
            )

        for k in range(devs):
            for r in range(CAP):
                copy_of(k, r).start()
        blocks = [acc_gu[:, c : c + width] for c in range(0, 2 * hidden, width)]
        blocks += [acc_out[:, c : c + width] for c in range(0, hidden, width)]
        blocks += [acc_td[...], jnp.concatenate([acc_gb[...], jnp.zeros((width - 16, width), F32)], axis=0)]
        half = len(blocks) // 2
        for i in range(half):
            rows_of = slice(i * width, (i + 1) * width)

            @pl.when(where_am[2] == 0)
            def _():
                keep[rows_of, :] = blocks[i]
                send[rows_of, :] = blocks[half + i]

            @pl.when(where_am[2] != 0)
            def _():
                keep[rows_of, :] = blocks[half + i]
                send[rows_of, :] = blocks[i]

        for k in range(devs):
            for r in range(CAP):
                copy_of(k, r).wait()


def heads_kernel(z_low, w_dist_t, out, wide):
    cols, bins, rows = out.shape
    wide[...] = z_low[...].astype(F32)

    def one(j, unused):
        column = wide[pl.ds(j, rows, stride=cols), :].astype(BF16)
        out[j] = dot_nt(w_dist_t[...], column).astype(BF16)
        return unused

    lax.fori_loop(0, cols, one, 0, unroll=8)


def logits_kernel(where_am, heads, got_a, got_b, out):
    straight = where_am[1] == 0
    low = low_lanes(heads.shape[1:])

    def one(p, unused):
        a, b = got_a[p].astype(F32), got_b[p].astype(F32)
        front, back = jnp.where(straight, a, b), jnp.where(straight, b, a)
        even = jnp.where(low, front, pltpu.roll(back, LANES // 2, 1))
        odd = jnp.where(low, pltpu.roll(front, LANES // 2, 1), back)
        out[2 * p] = (heads[2 * p].astype(F32) + even).astype(BF16)
        out[2 * p + 1] = (heads[2 * p + 1].astype(F32) + odd).astype(BF16)
        return unused

    lax.fori_loop(0, heads.shape[0] // 2, one, 0, unroll=4)


def tiles_kernel(devs, where_am, target, count, *refs):
    returned, (out, source) = refs[:devs], refs[devs:]
    feature, cells = out.shape[1:]
    groups = cells // LANES
    fill_slots(where_am[0], target, source, devs)
    for k in range(devs):
        for r in range(CAP):
            slot = source[k * CAP + r]

            @pl.when(slot >= 0)
            def _():
                scale = 1.0 / jnp.full((1, LANES), count[slot].astype(F32), F32)
                for c in range(groups):
                    at = (r * groups + c) * feature
                    part = returned[k][at : at + feature, :].astype(F32) * scale
                    out[slot, :, c * LANES : (c + 1) * LANES] = part.astype(BF16)


def weights_kernel(scale, where_am, mine, other, *outs):
    g_template, g_gain, g_bias, g_gate, g_up, g_out, g_dist = outs
    width, hidden = g_gate.shape
    feature = g_template.shape[0]
    half = mine.shape[0] // width
    lead = where_am[2] == 0
    per = hidden // width

    def block(i):
        source = slice(i % half * width, (i % half + 1) * width)
        here, there = mine[source, :], other[source, :]
        return (jnp.where(lead, here, there) if i < half else jnp.where(lead, there, here)) * scale

    for c in range(per):
        at = slice(c * width, (c + 1) * width)
        g_gate[:, at] = block(c)
        g_up[:, at] = block(per + c)
        g_out[at, :] = block(2 * per + c).T
    both = block(3 * per)
    g_template[...] = both[:feature, :]
    g_dist[...] = both[feature:, :]
    last = block(3 * per + 1)
    g_gain[...] = jnp.sum(last[0:8, :], axis=0, keepdims=True)
    g_bias[...] = jnp.sum(last[8:16, :], axis=0, keepdims=True)


def axis_groups(first, last):
    groups, bit = [], first
    while bit < last:
        wide = 2 if (last - bit) % 2 == 0 or last - bit > 2 else 1
        if (last - bit) % 2 == 1:
            wide = 1
        groups.append([m << bit for m in range(1, 1 << wide)])
        bit += wide
    return groups


def exchange_sum(value, axis, masks):
    size = lax.axis_size(axis)
    low = value.astype(BF16)
    got = [lax.ppermute(low, axis, [(i, i ^ m) for i in range(size)]) for m in masks]
    terms = [low.astype(F32)] + [g.astype(F32) for g in got]
    while len(terms) > 1:
        terms = [terms[i] + terms[i + 1] for i in range(0, len(terms), 2)]
    return terms[0]


def per_device(
    pair,
    logit_cotangent,
    tiles,
    tile_target,
    tile_square,
    tile_count,
    w_template,
    transition_norm_gain,
    transition_norm_bias,
    w_gate,
    w_up,
    w_out,
    w_dist,
):
    row_devs = lax.axis_size("row")
    col_devs = lax.axis_size("col")
    rows, cols, width = pair.shape
    bins = w_dist.shape[1]
    hidden = w_gate.shape[1]
    slots, cells_sq, feature = tiles.shape
    groups = cells_sq // LANES
    slab = groups * feature
    entries = rows * cols
    halves = rows // cols
    my_row, my_col = lax.axis_index("row"), lax.axis_index("col")
    where_am = jnp.stack([my_col, my_col % halves, my_row % 2]).astype(jnp.int32)
    target = tile_target[:, 0]
    tiles_t = jnp.transpose(tiles, (0, 2, 1))
    cot_t = jnp.transpose(logit_cotangent, (1, 2, 0))
    w_dist_t = w_dist.T

    def mirror(values):
        moved = []
        for s, value in enumerate(values):
            perm = [
                (r * col_devs + c, (c // halves) * col_devs + halves * r + ((c % halves) ^ s))
                for r in range(row_devs)
                for c in range(col_devs)
            ]
            moved.append(lax.ppermute(value, ("row", "col"), perm))
        return moved

    def shifted(values, sign):
        return [values[0]] + [
            lax.ppermute(values[k], "col", [(i, (i + sign * k) % col_devs) for i in range(col_devs)])
            for k in range(1, col_devs)
        ]

    half_shape = jax.ShapeDtypeStruct((cols // 2, bins, LANES), BF16)
    packed = pl.pallas_call(
        functools.partial(pack_kernel, col_devs),
        out_shape=[jax.ShapeDtypeStruct((CAP * slab + META, LANES), BF16)] * col_devs + [half_shape] * 2,
        in_specs=[SMEM] * 4 + [VMEM] * 2,
        out_specs=[VMEM] * (col_devs + 2),
        scratch_shapes=[pltpu.SMEM((col_devs * CAP,), jnp.int32)],
        compiler_params=params(),
        name="pack",
    )(where_am, target, tile_square, tile_count, tiles_t, cot_t)
    payloads = shifted(packed[:col_devs], 1)
    got_cot = mirror(packed[col_devs:])

    dheads = pl.pallas_call(
        cotangent_kernel,
        out_shape=jax.ShapeDtypeStruct((entries, bins), BF16),
        in_specs=[SMEM] + [VMEM] * 3,
        out_specs=VMEM,
        scratch_shapes=[pltpu.VMEM((entries, LANES), F32)],
        compiler_params=params(),
        name="cotangent",
    )(where_am, cot_t, *got_cot)

    block = STEP_ROWS * cols
    steps = entries // block
    squares = entries // cells_sq
    per_step = lambda lanes: pl.BlockSpec((block, lanes), lambda t: (t, 0))
    whole = lambda *shape: pl.BlockSpec(shape, lambda t: (0,) * len(shape))
    blocks = 3 * hidden // width + 2
    sum_shape = (blocks // 2 * width, width)
    operands = (
        w_template,
        transition_norm_gain[None, :],
        transition_norm_bias[None, :],
        w_gate,
        w_up,
        w_out,
        w_gate.T,
        w_up.T,
        w_out.T,
        w_dist_t,
    )
    outs = pl.pallas_call(
        functools.partial(main_kernel, col_devs, cols),
        grid=(steps,),
        out_shape=[
            jax.ShapeDtypeStruct((entries, width), F32),
            jax.ShapeDtypeStruct((entries, width), BF16),
            half_shape,
            half_shape,
        ]
        + [jax.ShapeDtypeStruct((CAP * slab, LANES), BF16)] * col_devs
        + [jax.ShapeDtypeStruct(sum_shape, F32)] * 2,
        in_specs=[SMEM]
        + [whole(CAP * slab + META, LANES)] * col_devs
        + [per_step(width), per_step(bins)]
        + [whole(*operand.shape) for operand in operands],
        out_specs=[per_step(width), per_step(width), whole(*half_shape.shape), whole(*half_shape.shape)]
        + [ANY] * col_devs
        + [whole(*sum_shape)] * 2,
        scratch_shapes=[
            pltpu.SMEM((col_devs * CAP,), jnp.int32),
            pltpu.VMEM((squares * slab, LANES), F32),
            pltpu.VMEM((squares * slab, LANES), BF16),
            pltpu.VMEM((squares, slab, LANES), BF16),
            pltpu.VMEM((width, 2 * hidden), F32),
            pltpu.VMEM((width, hidden), F32),
            pltpu.VMEM((feature + bins, width), F32),
            pltpu.VMEM((16, width), F32),
            pltpu.VMEM((block, 2 * hidden), BF16),
            pltpu.VMEM((block, hidden), BF16),
            pltpu.SemaphoreType.DMA((col_devs * CAP,)),
        ],
        compiler_params=params(),
        name="transition",
    )(where_am, *payloads, pair.reshape(entries, width), dheads, *operands)
    grad_pair, z_low, heads_a, heads_b = outs[:4]
    returns = outs[4 : 4 + col_devs]
    keep, send = outs[4 + col_devs :]

    sums = keep + lax.ppermute(send, "row", [(i, i ^ 1) for i in range(row_devs)])
    got_heads = mirror([heads_a, heads_b])
    returned = shifted(returns, -1)
    for axis, first, size in (("row", 1, row_devs), ("col", 0, col_devs)):
        for masks in axis_groups(first, size.bit_length() - 1):
            sums = exchange_sum(sums, axis, masks)
    other = lax.ppermute(sums, "row", [(i, i ^ 1) for i in range(row_devs)])

    heads = pl.pallas_call(
        heads_kernel,
        out_shape=jax.ShapeDtypeStruct((cols, bins, rows), BF16),
        in_specs=[VMEM] * 2,
        out_specs=VMEM,
        scratch_shapes=[pltpu.VMEM((entries, width), F32)],
        compiler_params=params(),
        name="own_heads",
    )(z_low, w_dist_t)
    logits = pl.pallas_call(
        logits_kernel,
        out_shape=jax.ShapeDtypeStruct((cols, bins, rows), BF16),
        in_specs=[SMEM] + [VMEM] * 3,
        out_specs=VMEM,
        compiler_params=params(),
        name="logits",
    )(where_am, heads, *got_heads)
    grad_tiles = pl.pallas_call(
        functools.partial(tiles_kernel, col_devs),
        out_shape=jax.ShapeDtypeStruct((slots, feature, cells_sq), BF16),
        in_specs=[SMEM] * 3 + [VMEM] * col_devs,
        out_specs=VMEM,
        scratch_shapes=[pltpu.SMEM((col_devs * CAP,), jnp.int32)],
        compiler_params=params(),
        name="tile_gradients",
    )(where_am, target, tile_count, *returned)
    length = rows * row_devs
    weights = pl.pallas_call(
        functools.partial(weights_kernel, 1.0 / length),
        out_shape=[
            jax.ShapeDtypeStruct((feature, width), F32),
            jax.ShapeDtypeStruct((1, width), F32),
            jax.ShapeDtypeStruct((1, width), F32),
            jax.ShapeDtypeStruct((width, hidden), F32),
            jax.ShapeDtypeStruct((width, hidden), F32),
            jax.ShapeDtypeStruct((hidden, width), F32),
            jax.ShapeDtypeStruct((bins, width), F32),
        ],
        in_specs=[SMEM] + [VMEM] * 2,
        out_specs=[VMEM] * 7,
        compiler_params=params(),
        name="weight_gradients",
    )(where_am, sums, other)
    g_template, g_gain, g_bias, g_gate, g_up, g_out, g_dist = weights
    return (
        jnp.transpose(logits, (2, 0, 1)),
        grad_pair.reshape(rows, cols, width),
        jnp.transpose(grad_tiles, (0, 2, 1)),
        g_template,
        g_gain[0],
        g_bias[0],
        g_gate,
        g_up,
        g_out,
        g_dist.T,
    )


def solution(mesh):
    split = P("row", "col", None)
    held = P(("row", "col"), None, None)
    return jax.shard_map(
        per_device,
        mesh=mesh,
        in_specs=(split, split, held, P(("row", "col"), None), P(("row", "col")), P(("row", "col")))
        + (P(),) * 7,
        out_specs=(split, split, held) + (P(),) * 7,
        check_vma=False,
    )
```

```python
import functools

import jax
import jax.numpy as jnp
from jax import lax
from jax.experimental import pallas as pl
from jax.experimental.pallas import tpu as pltpu
from jax.sharding import PartitionSpec as P

SQ = 32
CAP = 2
LANES = 128
META = 16
GROUP = LANES // SQ
PARTS = 2
PIECE = 256
VMEM_BYTES = 52 * 2**20
BF16 = jnp.bfloat16
F32 = jnp.float32

VMEM = pl.BlockSpec(memory_space=pltpu.VMEM)
SMEM = pl.BlockSpec(memory_space=pltpu.SMEM)
ANY = pl.BlockSpec(memory_space=pl.ANY)


def params():
    return pltpu.CompilerParams(vmem_limit_bytes=VMEM_BYTES)


def cost(micros):
    return pl.CostEstimate(flops=int(micros * 1.1e9), bytes_accessed=0, transcendentals=0)


def dot_nn(a, b):
    return lax.dot_general(a, b, (((1,), (0,)), ((), ())), preferred_element_type=F32)


def dot_nt(a, b):
    return lax.dot_general(a, b, (((1,), (1,)), ((), ())), preferred_element_type=F32)


def dot_tn(a, b):
    return lax.dot_general(a, b, (((0,), (0,)), ((), ())), preferred_element_type=F32)


def fill_slots(target, source, devs):
    def clear(i, unused):
        source[i] = -1
        return unused

    def place(s, unused):
        place_of = target[s] * CAP
        taken = source[place_of] >= 0
        source[place_of + jnp.where(taken, 1, 0)] = s
        return unused

    lax.fori_loop(0, devs * CAP, clear, 0)
    lax.fori_loop(0, target.shape[0], place, 0)


def low_lanes(shape):
    return lax.broadcasted_iota(jnp.int32, shape, 1) < LANES // 2


def pack_kernel(devs, where_am, target, square, count, tiles, cot, *refs):
    payloads, (cot_a, cot_b, source) = refs[:PARTS], refs[PARTS:]
    feature, cells = tiles.shape[1:]
    groups = cells // LANES
    per_part = groups // PARTS
    fill_slots(target, source, devs)
    first = where_am[0] == 0
    low = low_lanes(cot.shape[1:])

    def pack_pair(p, unused):
        even, odd = cot[2 * p].astype(F32), cot[2 * p + 1].astype(F32)
        front = jnp.where(low, even, pltpu.roll(odd, LANES // 2, 1)).astype(BF16)
        back = jnp.where(low, pltpu.roll(even, LANES // 2, 1), odd).astype(BF16)
        cot_a[p] = jnp.where(first, front, back)
        cot_b[p] = jnp.where(first, back, front)
        return unused

    lax.fori_loop(0, cot.shape[0] // 2, pack_pair, 0, unroll=4)
    line = lax.broadcasted_iota(jnp.int32, (META, LANES), 0)
    for k in range(devs):
        meta = jnp.zeros((META, LANES), F32)
        for r in range(CAP):
            slot = source[k * CAP + r]
            held = jnp.maximum(slot, 0)
            ident = jnp.where(slot >= 0, square[held], -1).astype(F32)
            meta = jnp.where(line == r, ident, meta)
            meta = jnp.where(line == 8 + r, count[held].astype(F32), meta)
            for c in range(groups):
                at = (r * per_part + c % per_part) * feature
                payloads[c // per_part][k, at : at + feature, :] = tiles[held, :, c * LANES : (c + 1) * LANES]
        for payload in payloads:
            payload[k, CAP * per_part * feature :, :] = meta.astype(BF16)


def arrived(where_am, direct, routed, p):
    return jnp.where(where_am[2] != 0, routed[p].astype(F32), direct[p].astype(F32))


def turn_kernel(cot, out, turned):
    cols, bins, rows = cot.shape

    def turn(j, unused):
        turned[pl.ds(j, rows, stride=cols), 0:bins] = cot[j].astype(F32).T
        return unused

    lax.fori_loop(0, cols, turn, 0, unroll=4)
    out[...] = turned[:, 0:bins].astype(BF16)


def fold_rows(values):
    return jnp.sum(values.reshape(values.shape[0] // 8, 8, values.shape[1]), axis=0)


def share_out(where_am, sums, keep, send):
    acc_gu, acc_out, acc_td, acc_gb = sums
    width = acc_gu.shape[0]
    blocks = [acc_gu[:, c : c + width] for c in range(0, acc_gu.shape[1], width)]
    blocks += [acc_out[:, c : c + width] for c in range(0, acc_out.shape[1], width)]
    blocks += [acc_td[...], jnp.concatenate([acc_gb[...], jnp.zeros((width - 16, width), F32)], axis=0)]
    half = len(blocks) // 2
    for i in range(half):
        rows = slice(i * width, (i + 1) * width)

        @pl.when(where_am[1] == 0)
        def _():
            keep[rows, :] = blocks[i]
            send[rows, :] = blocks[half + i]

        @pl.when(where_am[1] != 0)
        def _():
            keep[rows, :] = blocks[half + i]
            send[rows, :] = blocks[i]


def main_kernel(devs, cols, part, *refs):
    (where_am, payloads), refs = refs[:2], refs[2:]
    (pair, turned, got_a, got_b, got_c), refs = refs[:5], refs[5:]
    (w_template, gain, bias, w_gate, w_up, w_out, w_gate_t, w_up_t, w_out_t, w_dist_t), refs = refs[:10], refs[10:]
    last = part == PARTS - 1
    if part:
        carried, refs = refs[1:5], refs[5:]
    (grad_pair, z_low_out, heads_a, heads_b, returns), refs = refs[:5], refs[5:]
    if last:
        (keep, send), refs = refs[:2], refs[2:]
    acc_gu, acc_out, acc_td, acc_gb = sums = refs[:4]
    idents, total, summed, squares, low_gu, low_hid, sems = refs[4:]
    step = pl.program_id(0)
    steps = pl.num_programs(0)
    feature, width = w_template.shape
    hidden = w_gate.shape[1]
    groups = SQ * SQ // LANES
    slab = groups // PARTS * feature
    block = pair.shape[0]
    rows = block // cols
    sq_cols = cols // SQ
    per_part = groups // PARTS

    @pl.when(step == 0)
    def _():
        total[...] = jnp.zeros_like(total)
        for i, acc in enumerate(sums):
            acc[...] = carried[i][...] if part else jnp.zeros_like(acc)
        for k in range(devs):
            meta = payloads[k, CAP * slab :, :].astype(F32)
            for r in range(CAP):
                ident = jnp.max(meta[r : r + 1, :]).astype(jnp.int32)
                idents[k * CAP + r] = ident
                scale = 1.0 / meta[8 + r : 9 + r, :]

                @pl.when(ident >= 0)
                def _():
                    at = pl.multiple_of(ident * slab, slab)
                    total[pl.ds(at, slab), :] += payloads[k, r * slab : (r + 1) * slab, :].astype(F32) * scale

        summed[...] = total[...].astype(BF16)

    proj, pieces = [], []
    for c in range(per_part):
        across = []
        for s in range(sq_cols):
            at = pl.multiple_of(((step * sq_cols + s) * per_part + c) * feature, feature)
            piece = summed[pl.ds(at, feature), :]
            across.append(dot_tn(piece, w_template[...]).reshape(GROUP, SQ, width))
            pieces.append(piece)
        proj.append(jnp.concatenate(across, axis=1).reshape(GROUP * cols, width))
    z_one = pair[...] + jnp.concatenate(proj, axis=0)
    mean = jnp.mean(z_one, axis=1, keepdims=True)
    centred = z_one - mean
    deviation = lax.rsqrt(jnp.mean(centred * centred, axis=1, keepdims=True) + 1e-5)
    standard = centred * deviation
    normed = (standard * gain[...] + bias[...]).astype(BF16)
    per_half = steps // 2
    pairs = block // LANES
    at = lax.rem(step, per_half) * (PARTS * pairs) + part * pairs
    to = lax.rem(step, per_half) * pairs
    straight = step // per_half == where_am[0]
    mirrored = []
    for p in range(pairs):
        crossed = arrived(where_am, got_b, got_c, at + p)
        mirrored.append(jnp.where(straight, got_a[at + p].astype(F32), crossed).T)
    d_low = (turned[...].astype(F32) + jnp.concatenate(mirrored, axis=0)).astype(BF16)
    dz_two = dot_nn(d_low, w_dist_t[...])
    dz_low = dz_two.astype(BF16)

    z_two = z_one
    d_norm = jnp.zeros_like(z_one)
    for h in range(0, hidden, PIECE):
        e = h + PIECE
        gate = dot_nn(normed, w_gate[:, h:e])
        upper = dot_nn(normed, w_up[:, h:e])
        d_hidden = dot_nn(dz_low, w_out_t[:, h:e])
        sigma = 0.5 * jnp.tanh(0.5 * gate) + 0.5
        swish = gate * sigma
        hid = (swish * upper).astype(BF16)
        d_gate = (d_hidden * upper * (sigma + swish * (1.0 - sigma))).astype(BF16)
        d_upper = (d_hidden * swish).astype(BF16)
        z_two = z_two + dot_nn(hid, w_out[h:e, :])
        d_norm = d_norm + dot_nn(d_gate, w_gate_t[h:e, :]) + dot_nn(d_upper, w_up_t[h:e, :])
        low_hid[:, h:e] = hid
        low_gu[:, h:e] = d_gate
        low_gu[:, hidden + h : hidden + e] = d_upper

    acc_gu[...] += dot_tn(normed, low_gu[...])
    acc_out[...] += dot_tn(dz_low, low_hid[...])
    z_low = z_two.astype(BF16)
    z_low_out[...] = z_low
    acc_td[feature:, :] += dot_tn(d_low, z_low)
    acc_gb[0:8, :] += fold_rows(d_norm * standard)
    acc_gb[8:16, :] += fold_rows(d_norm)
    d_standard = d_norm * gain[...]
    grad = dz_two + deviation * (
        d_standard
        - jnp.mean(d_standard, axis=1, keepdims=True)
        - standard * jnp.mean(d_standard * standard, axis=1, keepdims=True)
    )
    grad_pair[...] = grad

    heads = dot_nt(w_dist_t[...], z_low).astype(BF16)

    @pl.when(straight)
    def _():
        for p in range(pairs):
            heads_a[to + p] = heads[:, p * LANES : (p + 1) * LANES]

    @pl.when(jnp.logical_not(straight))
    def _():
        for p in range(pairs):
            heads_b[to + p] = heads[:, p * LANES : (p + 1) * LANES]

    d_proj = grad.astype(BF16).reshape(rows, cols, width)
    for s in range(sq_cols):
        cells = d_proj[:, s * SQ : (s + 1) * SQ, :].reshape(rows * SQ, width)
        tile_grad = dot_nt(w_template[...], cells).astype(BF16)
        for c in range(per_part):
            squares[step * sq_cols + s, c * feature : (c + 1) * feature, :] = tile_grad[:, c * LANES : (c + 1) * LANES]
        side = jnp.concatenate([pieces[c * sq_cols + s] for c in range(per_part)], axis=1)
        acc_td[0:feature, :] += dot_nn(side, cells)

    @pl.when(step == steps - 1)
    def _():
        def copy_of(k, r):
            return pltpu.make_async_copy(
                squares.at[jnp.maximum(idents[k * CAP + r], 0)],
                returns.at[k, pl.ds(r * slab, slab)],
                sems.at[k * CAP + r],
            )

        for k in range(devs):
            for r in range(CAP):
                copy_of(k, r).start()
        if last:
            share_out(where_am, sums, keep, send)
        for k in range(devs):
            for r in range(CAP):
                copy_of(k, r).wait()


def heads_kernel(*refs):
    z_low, (w_dist_t, out, wide) = refs[:PARTS], refs[PARTS:]
    cols, bins, rows = out.shape
    block = SQ // PARTS * cols
    for part in range(PARTS):
        for band in range(rows // SQ):
            at = (band * PARTS + part) * block
            wide[at : at + block, :] = z_low[part][band * block : (band + 1) * block, :].astype(F32)

    def one(j, unused):
        column = wide[pl.ds(j, rows, stride=cols), :].astype(BF16)
        out[j] = dot_nt(w_dist_t[...], column).astype(BF16)
        return unused

    lax.fori_loop(0, cols, one, 0, unroll=8)


def logits_kernel(where_am, heads, *refs):
    got, out = refs[:-1], refs[-1]
    straight = where_am[0] == 0
    low = low_lanes(heads.shape[1:])
    per = SQ // PARTS // 2
    for part in range(PARTS):
        got_a, got_b, got_c = got[3 * part : 3 * part + 3]

        def one(p, unused):
            a, b = got_a[p].astype(F32), arrived(where_am, got_b, got_c, p)
            front, back = jnp.where(straight, a, b), jnp.where(straight, b, a)
            even = jnp.where(low, front, pltpu.roll(back, LANES // 2, 1))
            odd = jnp.where(low, pltpu.roll(front, LANES // 2, 1), back)
            at = p // per * SQ + part * (SQ // PARTS) + 2 * lax.rem(p, per)
            out[at] = (heads[at].astype(F32) + even).astype(BF16)
            out[at + 1] = (heads[at + 1].astype(F32) + odd).astype(BF16)
            return unused

        lax.fori_loop(0, got_a.shape[0], one, 0, unroll=4)


def tiles_kernel(devs, target, count, *refs):
    returned, (out, source) = refs[:PARTS], refs[PARTS:]
    feature, cells = out.shape[1:]
    groups = cells // LANES
    per_part = groups // PARTS
    fill_slots(target, source, devs)
    for k in range(devs):
        for r in range(CAP):
            slot = source[k * CAP + r]

            @pl.when(slot >= 0)
            def _():
                scale = 1.0 / jnp.full((1, LANES), count[slot].astype(F32), F32)
                for c in range(groups):
                    at = (r * per_part + c % per_part) * feature
                    piece = returned[c // per_part][k, at : at + feature, :].astype(F32) * scale
                    out[slot, :, c * LANES : (c + 1) * LANES] = piece.astype(BF16)


def weights_kernel(scale, where_am, mine, other, *outs):
    g_template, g_gain, g_bias, g_gate, g_up, g_out, g_dist = outs
    width, hidden = g_gate.shape
    feature = g_template.shape[0]
    half = mine.shape[0] // width
    lead = where_am[1] == 0
    per = hidden // width

    def block(i):
        source = slice(i % half * width, (i % half + 1) * width)
        here, there = mine[source, :].astype(F32), other[source, :].astype(F32)
        return (jnp.where(lead, here, there) if i < half else jnp.where(lead, there, here)) * scale

    for c in range(per):
        at = slice(c * width, (c + 1) * width)
        g_gate[:, at] = block(c)
        g_up[:, at] = block(per + c)
        g_out[at, :] = block(2 * per + c).T
    both = block(3 * per)
    g_template[...] = both[:feature, :]
    g_dist[...] = both[feature:, :]
    last = block(3 * per + 1)
    g_gain[...] = jnp.sum(last[0:8, :], axis=0, keepdims=True)
    g_bias[...] = jnp.sum(last[8:16, :], axis=0, keepdims=True)


def axis_groups(axis, first, size):
    last = size.bit_length() - 1
    groups, bit = [], first
    while bit < last:
        wide = 1 if (last - bit) % 2 else 2
        groups.append((axis, bit, [m << bit for m in range(1, 1 << wide)]))
        bit += wide
    return groups


def swap(value, axis, mask):
    return lax.ppermute(value, axis, [(i, i ^ mask) for i in range(lax.axis_size(axis))])


def all_sum(value, settle):
    groups = axis_groups("row", 1, lax.axis_size("row")) + axis_groups("col", 0, lax.axis_size("col"))
    pairs = [(axis, bit) for axis, bit, masks in groups if len(masks) == 1]
    split = []
    for axis, bit in pairs:
        mine = (lax.axis_index(axis) >> bit) & 1
        both = value.reshape(2, value.shape[0] // 2, value.shape[1])
        away = lax.dynamic_index_in_dim(both, 1 - mine, 0, False).astype(BF16)
        value = lax.dynamic_index_in_dim(both, mine, 0, False) + swap(away, axis, 1 << bit).astype(F32)
        split.append(mine)
    value = settle[0](value)
    for axis, bit, masks in groups:
        if len(masks) == 1:
            continue
        low = value.astype(BF16)
        terms = [low.astype(F32)] + [swap(low, axis, m).astype(F32) for m in masks]
        while len(terms) > 1:
            terms = [terms[i] + terms[i + 1] for i in range(0, len(terms), 2)]
        value = terms[0]
    low = settle[1](value.astype(BF16))
    for (axis, bit), mine in reversed(list(zip(pairs, split))):
        other = swap(low, axis, 1 << bit)
        low = jnp.where(mine == 0, jnp.concatenate([low, other]), jnp.concatenate([other, low]))
    return low


def per_device(
    pair,
    logit_cotangent,
    tiles,
    tile_target,
    tile_square,
    tile_count,
    w_template,
    transition_norm_gain,
    transition_norm_bias,
    w_gate,
    w_up,
    w_out,
    w_dist,
):
    row_devs = lax.axis_size("row")
    col_devs = lax.axis_size("col")
    rows, cols, width = pair.shape
    bins = w_dist.shape[1]
    hidden = w_gate.shape[1]
    slots, cells_sq, feature = tiles.shape
    groups = cells_sq // LANES
    slab = groups * feature
    entries = rows * cols
    halves = rows // cols
    my_row, my_col = lax.axis_index("row"), lax.axis_index("col")
    two_chips = row_devs == 4
    crosses = (my_col // halves // 2 != my_row // 2) & two_chips
    where_am = jnp.stack([my_col % halves, my_row % 2, crosses.astype(jnp.int32)]).astype(jnp.int32)
    target = tile_target[:, 0]
    tiles_t = jnp.transpose(tiles, (0, 2, 1))
    cot_t = jnp.transpose(logit_cotangent, (1, 2, 0))
    w_dist_t = w_dist.T

    def mirror(first, second):
        everywhere = [(r, c) for r in range(row_devs) for c in range(col_devs)]

        def move(value, steps):
            perm = [(a * col_devs + b, c * col_devs + d) for (a, b), (c, d) in steps]
            return lax.ppermute(value, ("row", "col"), perm)

        def ends(s):
            return [((r, c), (c // halves, halves * r + ((c % halves) ^ s))) for r, c in everywhere]

        direct = move(first, ends(0))
        if not two_chips:
            other = move(second, ends(1))
            return [direct, other, other], lambda value: value
        across = [((r, c), (e // 2 * 2 + r % 2, c), (e, f)) for (r, c), (e, f) in ends(1) if r // 2 != e // 2]
        stay = move(second, [(a, b) for a, b in ends(1) if a[0] // 2 == b[0] // 2])
        over = move(second, [(a, b) for a, b, c in across])
        return [direct, stay, over], lambda value: move(value, [(b, c) for a, b, c in across])

    def stacked(shape, dtype=BF16):
        return jax.ShapeDtypeStruct(shape, dtype)

    part_slab = slab // PARTS
    packed = pl.pallas_call(
        functools.partial(pack_kernel, col_devs),
        out_shape=[stacked((col_devs, CAP * part_slab + META, LANES))] * PARTS + [stacked((cols // 2, bins, LANES))] * 2,
        in_specs=[SMEM] * 4 + [VMEM] * 2,
        out_specs=[VMEM] * (PARTS + 2),
        scratch_shapes=[pltpu.SMEM((col_devs * CAP,), jnp.int32)],
        compiler_params=params(),
        cost_estimate=cost(5),
        name="pack",
    )(where_am, target, tile_square, tile_count, tiles_t, cot_t)
    payloads = list(packed[:PARTS])
    payloads[0] = lax.all_to_all(payloads[0], "col", 0, 0, tiled=True)
    (*got_cot, over), land = mirror(*packed[PARTS:])
    got_cot.append(land(over))
    payloads[1], *got_cot = lax.optimization_barrier((payloads[1], *got_cot))
    payloads[1] = lax.all_to_all(payloads[1], "col", 0, 0, tiled=True)

    turned = pl.pallas_call(
        turn_kernel,
        out_shape=stacked((entries, bins)),
        in_specs=[VMEM],
        out_specs=VMEM,
        scratch_shapes=[pltpu.VMEM((entries, LANES), F32)],
        compiler_params=params(),
        cost_estimate=cost(5),
        name="turn",
    )(cot_t)

    block = SQ // PARTS * cols
    steps = rows // SQ
    squares = entries // cells_sq
    whole = lambda *shape: pl.BlockSpec(shape, lambda t: (0,) * len(shape))
    blocks = 3 * hidden // width + 2
    sum_shape = (blocks // 2 * width, width)
    operands = (
        w_template,
        transition_norm_gain[None, :],
        transition_norm_bias[None, :],
        w_gate,
        w_up,
        w_out,
        w_gate.T,
        w_up.T,
        w_out.T,
        w_dist_t,
    )
    sums_shapes = [(width, 2 * hidden), (width, hidden), (feature + bins, width), (16, width)]
    half_heads = (cols // 2, bins, LANES)
    part_heads = (cols // 2 // PARTS, bins, LANES)
    pair_cells = pair.reshape(entries, width)

    def transition(part, before):
        last = part == PARTS - 1
        per_step = lambda lanes: pl.BlockSpec((block, lanes), lambda t: (PARTS * t + part, 0))
        out_shape = [
            stacked((entries, width), F32),
            stacked((entries // PARTS, width)),
            stacked(part_heads),
            stacked(part_heads),
            stacked((col_devs, CAP * part_slab, LANES)),
        ]
        out_specs = [
            per_step(width),
            pl.BlockSpec((block, width), lambda t: (t, 0)),
            whole(*part_heads),
            whole(*part_heads),
            ANY,
        ]
        scratch = [
            pltpu.SMEM((col_devs * CAP,), jnp.int32),
            pltpu.VMEM((squares * part_slab, LANES), F32),
            pltpu.VMEM((squares * part_slab, LANES), BF16),
            pltpu.VMEM((squares, part_slab, LANES), BF16),
            pltpu.VMEM((block, 2 * hidden), BF16),
            pltpu.VMEM((block, hidden), BF16),
            pltpu.SemaphoreType.DMA((col_devs * CAP,)),
        ]
        if last:
            out_shape += [stacked(sum_shape, F32)] * 2
            out_specs += [whole(*sum_shape)] * 2
            scratch = [pltpu.VMEM(shape, F32) for shape in sums_shapes] + scratch
        else:
            out_shape += [stacked(shape, F32) for shape in sums_shapes]
            out_specs += [whole(*shape) for shape in sums_shapes]
        inputs = (where_am, payloads[part], pair_cells, turned, *got_cot, *operands)
        in_specs = [SMEM, whole(col_devs, CAP * part_slab + META, LANES), per_step(width), per_step(bins)]
        in_specs += [whole(*half_heads)] * 3
        in_specs += [whole(*operand.shape) for operand in operands]
        aliases = {}
        if part:
            aliases = {len(inputs): 0}
            inputs += tuple(before)
            in_specs += [ANY] + [whole(*shape) for shape in sums_shapes]
        return pl.pallas_call(
            functools.partial(main_kernel, col_devs, cols, part),
            grid=(steps,),
            out_shape=out_shape,
            in_specs=in_specs,
            out_specs=out_specs,
            scratch_shapes=scratch,
            input_output_aliases=aliases,
            compiler_params=params(),
            cost_estimate=cost(20),
            name=f"transition_{part}",
        )(*inputs)

    before, z_low, got_heads, returned = None, [], [], []
    for part in range(PARTS):
        outs = transition(part, before)
        grad_pair = outs[0]
        before = (grad_pair, *outs[5:])
        z_low.append(outs[1])
        if part == PARTS - 1:
            keep, send, returned[0], *got_heads[0] = lax.optimization_barrier((*outs[5:], *returned, *got_heads[0]))
            got_heads[0][2] = land(got_heads[0][2])
            sums = keep + swap(send, "row", 1)
        got, land = mirror(outs[2], outs[3])
        got_heads.append(got)
        returned.append(lax.all_to_all(outs[4], "col", 0, 0, tiled=True))

    heads = pl.pallas_call(
        heads_kernel,
        out_shape=stacked((cols, bins, rows)),
        in_specs=[VMEM] * (PARTS + 1),
        out_specs=VMEM,
        scratch_shapes=[pltpu.VMEM((entries, width), F32)],
        compiler_params=params(),
        cost_estimate=cost(5),
        name="own_heads",
    )(*z_low, w_dist_t)

    own = [heads]

    def heads_sent(value):
        got = lax.optimization_barrier((value, *got_heads[1], got_heads[0][2]))
        got_heads[0][2] = got[4]
        got_heads[1] = [got[1], got[2], land(got[3])]
        return got[0]

    def heads_landed(value):
        value, own[0], returned[1] = lax.optimization_barrier((value, own[0], returned[1]))
        return value

    sums = all_sum(sums, (heads_sent, heads_landed))
    other = swap(sums, "row", 1)
    logits = pl.pallas_call(
        logits_kernel,
        out_shape=jax.ShapeDtypeStruct((cols, bins, rows), BF16),
        in_specs=[SMEM] + [VMEM] * (1 + 3 * PARTS),
        out_specs=VMEM,
        compiler_params=params(),
        cost_estimate=cost(3),
        name="logits",
    )(where_am, own[0], *got_heads[0], *got_heads[1])
    grad_tiles = pl.pallas_call(
        functools.partial(tiles_kernel, col_devs),
        out_shape=jax.ShapeDtypeStruct((slots, feature, cells_sq), BF16),
        in_specs=[SMEM] * 2 + [VMEM] * PARTS,
        out_specs=VMEM,
        scratch_shapes=[pltpu.SMEM((col_devs * CAP,), jnp.int32)],
        compiler_params=params(),
        cost_estimate=cost(4),
        name="tile_gradients",
    )(target, tile_count, *returned)
    length = rows * row_devs
    weights = pl.pallas_call(
        functools.partial(weights_kernel, 1.0 / length),
        out_shape=[
            jax.ShapeDtypeStruct((feature, width), F32),
            jax.ShapeDtypeStruct((1, width), F32),
            jax.ShapeDtypeStruct((1, width), F32),
            jax.ShapeDtypeStruct((width, hidden), F32),
            jax.ShapeDtypeStruct((width, hidden), F32),
            jax.ShapeDtypeStruct((hidden, width), F32),
            jax.ShapeDtypeStruct((bins, width), F32),
        ],
        in_specs=[SMEM] + [VMEM] * 2,
        out_specs=[VMEM] * 7,
        compiler_params=params(),
        cost_estimate=cost(2),
        name="weight_gradients",
    )(where_am, sums, other)
    g_template, g_gain, g_bias, g_gate, g_up, g_out, g_dist = weights
    return (
        jnp.transpose(logits, (2, 0, 1)),
        grad_pair.reshape(rows, cols, width),
        jnp.transpose(grad_tiles, (0, 2, 1)),
        g_template,
        g_gain[0],
        g_bias[0],
        g_gate,
        g_up,
        g_out,
        g_dist.T,
    )


def solution(mesh):
    split = P("row", "col", None)
    held = P(("row", "col"), None, None)
    return jax.shard_map(
        per_device,
        mesh=mesh,
        in_specs=(split, split, held, P(("row", "col"), None), P(("row", "col")), P(("row", "col")))
        + (P(),) * 7,
        out_specs=(split, split, held) + (P(),) * 7,
        check_vma=False,
    )
```

```python
import functools

import jax
import jax.numpy as jnp
from jax import lax
from jax.experimental import pallas as pl
from jax.experimental.pallas import tpu as pltpu
from jax.sharding import PartitionSpec as P

SQ = 32
CAP = 2
LANES = 128
META = 16
GROUP = LANES // SQ
PARTS = 2
PIECE = 256
VMEM_BYTES = 52 * 2**20
BF16 = jnp.bfloat16
F32 = jnp.float32

VMEM = pl.BlockSpec(memory_space=pltpu.VMEM)
SMEM = pl.BlockSpec(memory_space=pltpu.SMEM)
ANY = pl.BlockSpec(memory_space=pl.ANY)


def params():
    return pltpu.CompilerParams(vmem_limit_bytes=VMEM_BYTES)


def cost(micros):
    return pl.CostEstimate(flops=int(micros * 1.1e9), bytes_accessed=0, transcendentals=0)


def dot_nn(a, b):
    return lax.dot_general(a, b, (((1,), (0,)), ((), ())), preferred_element_type=F32)


def dot_nt(a, b):
    return lax.dot_general(a, b, (((1,), (1,)), ((), ())), preferred_element_type=F32)


def dot_tn(a, b):
    return lax.dot_general(a, b, (((0,), (0,)), ((), ())), preferred_element_type=F32)


def fill_slots(target, source, devs):
    def clear(i, unused):
        source[i] = -1
        return unused

    def place(s, unused):
        place_of = target[s] * CAP
        taken = source[place_of] >= 0
        source[place_of + jnp.where(taken, 1, 0)] = s
        return unused

    lax.fori_loop(0, devs * CAP, clear, 0)
    lax.fori_loop(0, target.shape[0], place, 0)


def low_lanes(shape):
    return lax.broadcasted_iota(jnp.int32, shape, 1) < LANES // 2


def pack_kernel(devs, target, square, count, tiles, payload, source, *scratch):
    *scalars, sems = scratch
    copies = [pltpu.make_async_copy(a, b, sems.at[i]) for i, (a, b) in enumerate(zip((target, square, count), scalars))]
    for copy in copies:
        copy.start()
    for copy in copies:
        copy.wait()
    target, square, count = scalars
    feature, cells = tiles.shape[1:]
    groups = cells // LANES
    fill_slots(target, source, devs)
    line = lax.broadcasted_iota(jnp.int32, (META, LANES), 0)
    for k in range(devs):
        meta = jnp.zeros((META, LANES), F32)
        for r in range(CAP):
            slot = source[k * CAP + r]
            held = jnp.maximum(slot, 0)
            ident = jnp.where(slot >= 0, square[held], -1).astype(F32)
            meta = jnp.where(line == r, ident, meta)
            meta = jnp.where(line == 8 + r, count[held].astype(F32), meta)
            for c in range(groups):
                at = (r * groups + c) * feature
                payload[k, at : at + feature, :] = tiles[held, :, c * LANES : (c + 1) * LANES]
        payload[k, CAP * groups * feature :, :] = meta.astype(BF16)


def pack_cotangent_kernel(where_am, cot, cot_a, cot_b):
    first = where_am[0] == 0
    low = low_lanes(cot.shape[1:])

    def pack_pair(p, unused):
        even, odd = cot[2 * p].astype(F32), cot[2 * p + 1].astype(F32)
        front = jnp.where(low, even, pltpu.roll(odd, LANES // 2, 1)).astype(BF16)
        back = jnp.where(low, pltpu.roll(even, LANES // 2, 1), odd).astype(BF16)
        cot_a[p] = jnp.where(first, front, back)
        cot_b[p] = jnp.where(first, back, front)
        return unused

    lax.fori_loop(0, cot.shape[0] // 2, pack_pair, 0, unroll=4)


def arrived(where_am, direct, routed, p):
    return jnp.where(where_am[2] != 0, routed[p].astype(F32), direct[p].astype(F32))


def turn_kernel(cot, out, turned):
    cols, bins, rows = cot.shape

    def turn(j, unused):
        turned[pl.ds(j, rows, stride=cols), 0:bins] = cot[j].astype(F32).T
        return unused

    lax.fori_loop(0, cols, turn, 0, unroll=4)
    out[...] = turned[:, 0:bins].astype(BF16)


def fold_rows(values):
    return jnp.sum(values.reshape(values.shape[0] // 8, 8, values.shape[1]), axis=0)


def share_out(where_am, sums, keep, send):
    acc_gu, acc_out, acc_td, acc_gb = sums
    width = acc_gu.shape[0]
    blocks = [acc_gu[:, c : c + width] for c in range(0, acc_gu.shape[1], width)]
    blocks += [acc_out[:, c : c + width] for c in range(0, acc_out.shape[1], width)]
    blocks += [acc_td[...], jnp.concatenate([acc_gb[...], jnp.zeros((width - 16, width), F32)], axis=0)]
    half = len(blocks) // 2
    for i in range(half):
        rows = slice(i * width, (i + 1) * width)

        @pl.when(where_am[1] == 0)
        def _():
            keep[rows, :] = blocks[i]
            send[rows, :] = blocks[half + i]

        @pl.when(where_am[1] != 0)
        def _():
            keep[rows, :] = blocks[half + i]
            send[rows, :] = blocks[i]


def main_kernel(devs, cols, part, *refs):
    (where_am, payloads), refs = refs[:2], refs[2:]
    (pair, turned, got_a, got_b, got_c), refs = refs[:5], refs[5:]
    (w_template, gain, bias, w_gate, w_up, w_out, w_gate_t, w_up_t, w_out_t, w_dist_t), refs = refs[:10], refs[10:]
    last = part == PARTS - 1
    if part:
        carried, refs = refs[1:5], refs[5:]
    (grad_pair, z_low_out, heads_a, heads_b, returns), refs = refs[:5], refs[5:]
    if last:
        (keep, send), refs = refs[:2], refs[2:]
    acc_gu, acc_out, acc_td, acc_gb = sums = refs[:4]
    idents, total, summed, squares, low_gu, low_hid, sems = refs[4:]
    step = pl.program_id(0)
    steps = pl.num_programs(0)
    feature, width = w_template.shape
    hidden = w_gate.shape[1]
    groups = SQ * SQ // LANES
    slab = groups // PARTS * feature
    block = pair.shape[0]
    rows = block // cols
    sq_cols = cols // SQ
    per_part = groups // PARTS

    @pl.when(step == 0)
    def _():
        total[...] = jnp.zeros_like(total)
        for i, acc in enumerate(sums):
            acc[...] = carried[i][...] if part else jnp.zeros_like(acc)
        metas = [payloads[k, CAP * slab :, :].astype(F32) for k in range(devs)]
        tops = [(k, r, jnp.max(metas[k][r : r + 1, :])) for k in range(devs) for r in range(CAP)]
        for k, r, top in tops:
            ident = top.astype(jnp.int32)
            idents[k * CAP + r] = ident
            scale = jnp.where(metas[k][r : r + 1, :] >= 0, 1.0 / metas[k][8 + r : 9 + r, :], 0.0)
            at = pl.multiple_of(jnp.maximum(ident, 0) * slab, slab)
            total[pl.ds(at, slab), :] += payloads[k, r * slab : (r + 1) * slab, :].astype(F32) * scale

        summed[...] = total[...].astype(BF16)

    proj, pieces = [], []
    for c in range(per_part):
        across = []
        for s in range(sq_cols):
            at = pl.multiple_of(((step * sq_cols + s) * per_part + c) * feature, feature)
            piece = summed[pl.ds(at, feature), :]
            across.append(dot_tn(piece, w_template[...]).reshape(GROUP, SQ, width))
            pieces.append(piece)
        proj.append(jnp.concatenate(across, axis=1).reshape(GROUP * cols, width))
    z_one = pair[...] + jnp.concatenate(proj, axis=0)
    mean = jnp.mean(z_one, axis=1, keepdims=True)
    centred = z_one - mean
    deviation = lax.rsqrt(jnp.mean(centred * centred, axis=1, keepdims=True) + 1e-5)
    standard = centred * deviation
    normed = (standard * gain[...] + bias[...]).astype(BF16)
    per_half = steps // 2
    pairs = block // LANES
    to = lax.rem(step, per_half) * pairs
    straight = step // per_half == where_am[0]
    mirrored = []
    for p in range(pairs):
        crossed = arrived(where_am, got_b, got_c, p)
        mirrored.append(jnp.where(straight, got_a[p].astype(F32), crossed).T)
    d_low = (turned[...].astype(F32) + jnp.concatenate(mirrored, axis=0)).astype(BF16)
    dz_two = dot_nn(d_low, w_dist_t[...])
    dz_low = dz_two.astype(BF16)

    z_two = z_one
    d_norm = jnp.zeros_like(z_one)
    for h in range(0, hidden, PIECE):
        e = h + PIECE
        gate = dot_nn(normed, w_gate[:, h:e])
        upper = dot_nn(normed, w_up[:, h:e])
        d_hidden = dot_nn(dz_low, w_out_t[:, h:e])
        sigma = 0.5 * jnp.tanh(0.5 * gate) + 0.5
        swish = gate * sigma
        hid = (swish * upper).astype(BF16)
        d_gate = (d_hidden * upper * (sigma + swish * (1.0 - sigma))).astype(BF16)
        d_upper = (d_hidden * swish).astype(BF16)
        z_two = z_two + dot_nn(hid, w_out[h:e, :])
        d_norm = d_norm + dot_nn(d_gate, w_gate_t[h:e, :]) + dot_nn(d_upper, w_up_t[h:e, :])
        low_hid[:, h:e] = hid
        low_gu[:, h:e] = d_gate
        low_gu[:, hidden + h : hidden + e] = d_upper

    acc_gu[...] += dot_tn(normed, low_gu[...])
    acc_out[...] += dot_tn(dz_low, low_hid[...])
    z_low = z_two.astype(BF16)
    z_low_out[...] = z_low
    acc_td[feature:, :] += dot_tn(d_low, z_low)
    acc_gb[0:8, :] += fold_rows(d_norm * standard)
    acc_gb[8:16, :] += fold_rows(d_norm)
    d_standard = d_norm * gain[...]
    grad = dz_two + deviation * (
        d_standard
        - jnp.mean(d_standard, axis=1, keepdims=True)
        - standard * jnp.mean(d_standard * standard, axis=1, keepdims=True)
    )
    grad_pair[...] = grad

    heads = dot_nt(w_dist_t[...], z_low).astype(BF16)

    @pl.when(straight)
    def _():
        for p in range(pairs):
            heads_a[to + p] = heads[:, p * LANES : (p + 1) * LANES]

    @pl.when(jnp.logical_not(straight))
    def _():
        for p in range(pairs):
            heads_b[to + p] = heads[:, p * LANES : (p + 1) * LANES]

    d_proj = grad.astype(BF16).reshape(rows, cols, width)
    for s in range(sq_cols):
        cells = d_proj[:, s * SQ : (s + 1) * SQ, :].reshape(rows * SQ, width)
        tile_grad = dot_nt(w_template[...], cells).astype(BF16)
        for c in range(per_part):
            squares[step * sq_cols + s, c * feature : (c + 1) * feature, :] = tile_grad[:, c * LANES : (c + 1) * LANES]
        side = jnp.concatenate([pieces[c * sq_cols + s] for c in range(per_part)], axis=1)
        acc_td[0:feature, :] += dot_nn(side, cells)

    @pl.when(step == steps - 1)
    def _():
        def copy_of(k, r):
            return pltpu.make_async_copy(
                squares.at[jnp.maximum(idents[k * CAP + r], 0)],
                returns.at[k, pl.ds(r * slab, slab)],
                sems.at[k * CAP + r],
            )

        for k in range(devs):
            for r in range(CAP):
                copy_of(k, r).start()
        if last:
            share_out(where_am, sums, keep, send)
        for k in range(devs):
            for r in range(CAP):
                copy_of(k, r).wait()


def heads_kernel(*refs):
    z_low, (w_dist_t, out, wide) = refs[:PARTS], refs[PARTS:]
    cols, bins, rows = out.shape
    block = SQ // PARTS * cols
    for part in range(PARTS):
        for band in range(rows // SQ):
            at = (band * PARTS + part) * block
            wide[at : at + block, :] = z_low[part][band * block : (band + 1) * block, :].astype(F32)

    def one(j, unused):
        column = wide[pl.ds(j, rows, stride=cols), :].astype(BF16)
        out[j] = dot_nt(w_dist_t[...], column).astype(BF16)
        return unused

    lax.fori_loop(0, cols, one, 0, unroll=8)


def logits_kernel(where_am, heads, got_a, got_b, got_c, *refs):
    out = refs[-1]
    straight = where_am[0] == 0
    low = low_lanes(heads.shape[1:])
    for p in range(got_a.shape[0]):
        a, b = got_a[p].astype(F32), arrived(where_am, got_b, got_c, p)
        front, back = jnp.where(straight, a, b), jnp.where(straight, b, a)
        even = jnp.where(low, front, pltpu.roll(back, LANES // 2, 1))
        odd = jnp.where(low, pltpu.roll(front, LANES // 2, 1), back)
        out[2 * p] = (heads[2 * p].astype(F32) + even).astype(BF16)
        out[2 * p + 1] = (heads[2 * p + 1].astype(F32) + odd).astype(BF16)


def tiles_kernel(devs, target, count, returned, *refs):
    out, source = refs[-2:]
    feature, cells = out.shape[1:]
    groups = cells // LANES
    fill_slots(target, source, devs)
    for k in range(devs):
        for r in range(CAP):
            slot = source[k * CAP + r]

            @pl.when(slot >= 0)
            def _():
                scale = 1.0 / jnp.full((1, LANES), count[slot].astype(F32), F32)
                for c in range(groups):
                    at = (r * groups + c) * feature
                    piece = returned[k, at : at + feature, :].astype(F32) * scale
                    out[slot, :, c * LANES : (c + 1) * LANES] = piece.astype(BF16)


def weights_kernel(scale, where_am, *refs):
    pieces, (g_template, g_gain, g_bias, g_gate, g_up, g_out, g_dist, total) = refs[:-8], refs[-8:]
    width, hidden = g_gate.shape
    feature = g_template.shape[0]
    per = hidden // width
    rows = pieces[0].shape[0] // 2
    half = rows * len(pieces)
    for m, piece in enumerate(pieces):
        for core in range(2):
            at = (where_am[1] ^ core) * half + (where_am[3] ^ m) * rows
            there = pl.ds(pl.multiple_of(at, 32), rows)
            total[there, :] = piece[core * rows : (core + 1) * rows, :].astype(F32) * scale

    def block(i):
        return total[i * width : (i + 1) * width, :]

    for c in range(per):
        at = slice(c * width, (c + 1) * width)
        g_gate[:, at] = block(c)
        g_up[:, at] = block(per + c)
        g_out[at, :] = block(2 * per + c).T
    both = block(3 * per)
    g_template[...] = both[:feature, :]
    g_dist[...] = both[feature:, :]
    last = block(3 * per + 1)
    g_gain[...] = jnp.sum(last[0:8, :], axis=0, keepdims=True)
    g_bias[...] = jnp.sum(last[8:16, :], axis=0, keepdims=True)


def axis_groups(axis, first, size):
    last = size.bit_length() - 1
    groups, bit = [], first
    while bit < last:
        wide = 1 if (last - bit) % 2 else 2
        groups.append((axis, bit, [m << bit for m in range(1, 1 << wide)]))
        bit += wide
    return groups


def swap(value, axis, mask):
    return lax.ppermute(value, axis, [(i, i ^ mask) for i in range(lax.axis_size(axis))])


def all_sum(value, settle):
    groups = axis_groups("row", 1, lax.axis_size("row")) + axis_groups("col", 0, lax.axis_size("col"))
    pairs = [(axis, bit) for axis, bit, masks in groups if len(masks) == 1]
    split = []
    for axis, bit in pairs:
        mine = (lax.axis_index(axis) >> bit) & 1
        both = value.reshape(2, value.shape[0] // 2, value.shape[1])
        away = lax.dynamic_index_in_dim(both, 1 - mine, 0, False).astype(BF16)
        value = lax.dynamic_index_in_dim(both, mine, 0, False) + swap(away, axis, 1 << bit).astype(F32)
        split.append(mine)
    value = settle[0](value)
    for axis, bit, masks in groups:
        if len(masks) == 1:
            continue
        low = value.astype(BF16)
        terms = [low.astype(F32)] + [swap(low, axis, m).astype(F32) for m in masks]
        while len(terms) > 1:
            terms = [terms[i] + terms[i + 1] for i in range(0, len(terms), 2)]
        value = terms[0]
    low = settle[1](value.astype(BF16))
    for (axis, bit), mine in reversed(list(zip(pairs, split))):
        other = swap(low, axis, 1 << bit)
        low = jnp.where(mine == 0, jnp.concatenate([low, other]), jnp.concatenate([other, low]))
    return low


def split_kernel(where_am, keep, got, mine, *sends):
    rows = mine.shape[0]
    for m, out in enumerate((mine, *sends)):
        at = pl.multiple_of((where_am[3] ^ m) * rows, 32)
        out[...] = (keep[pl.ds(at, rows), :] + got[pl.ds(at, rows), :]).astype(out.dtype)


def flip(value, m):
    rows, cols = lax.axis_size("row"), lax.axis_size("col")
    perm = [(r * cols + c, (r ^ (m & 2)) * cols + (c ^ (m & 1))) for r in range(rows) for c in range(cols)]
    return lax.ppermute(value, ("row", "col"), perm)


def all_sum_four(where_am, keep, got, settle):
    rows, width = keep.shape[0] // 4, keep.shape[1]
    mine, *sends = pl.pallas_call(
        split_kernel,
        out_shape=[jax.ShapeDtypeStruct((rows, width), F32 if m == 0 else BF16) for m in range(4)],
        in_specs=[SMEM] + [VMEM] * 2,
        out_specs=[VMEM] * 4,
        compiler_params=params(),
        cost_estimate=cost(1),
        name="split_sums",
    )(where_am, keep, got)
    a, b, c = [flip(send, m + 1).astype(F32) for m, send in enumerate(sends)]
    low = settle[0](((mine + a) + (b + c)).astype(BF16))
    a, b, c = [swap(low, "col", m).astype(F32) for m in (2, 4, 6)]
    low = settle[1](((low.astype(F32) + a) + (b + c)).astype(BF16))
    both = jnp.concatenate([low, swap(low, "row", 1)])
    return [both] + [flip(both, m) for m in (1, 2, 3)]


def per_device(
    pair,
    logit_cotangent,
    tiles,
    tile_target,
    tile_square,
    tile_count,
    w_template,
    transition_norm_gain,
    transition_norm_bias,
    w_gate,
    w_up,
    w_out,
    w_dist,
):
    row_devs = lax.axis_size("row")
    col_devs = lax.axis_size("col")
    rows, cols, width = pair.shape
    bins = w_dist.shape[1]
    hidden = w_gate.shape[1]
    slots, cells_sq, feature = tiles.shape
    groups = cells_sq // LANES
    slab = groups * feature
    entries = rows * cols
    halves = rows // cols
    my_row, my_col = lax.axis_index("row"), lax.axis_index("col")
    two_chips = row_devs == 4
    crosses = (my_col // halves // 2 != my_row // 2) & two_chips
    quarter = jnp.where(two_chips, my_row // 2 * 2 + my_col % 2, 0)
    where_am = jnp.stack([my_col % halves, my_row % 2, crosses.astype(jnp.int32), quarter]).astype(jnp.int32)
    target = tile_target[:, 0]
    tiles_t = jnp.transpose(tiles, (0, 2, 1))
    cot_t = jnp.transpose(logit_cotangent, (1, 2, 0))
    w_dist_t = w_dist.T

    def mirror(first, second):
        everywhere = [(r, c) for r in range(row_devs) for c in range(col_devs)]

        def move(value, steps):
            perm = [(a * col_devs + b, c * col_devs + d) for (a, b), (c, d) in steps]
            return lax.ppermute(value, ("row", "col"), perm)

        def ends(s):
            return [((r, c), (c // halves, halves * r + ((c % halves) ^ s))) for r, c in everywhere]

        direct = move(first, ends(0))
        if not two_chips:
            other = move(second, ends(1))
            return [direct, other, other], lambda value: value
        across = [((r, c), (e // 2 * 2 + r % 2, c), (e, f)) for (r, c), (e, f) in ends(1) if r // 2 != e // 2]
        stay = move(second, [(a, b) for a, b in ends(1) if a[0] // 2 == b[0] // 2])
        over = move(second, [(a, b) for a, b, c in across])
        return [direct, stay, over], lambda value: move(value, [(b, c) for a, b, c in across])

    def stacked(shape, dtype=BF16):
        return jax.ShapeDtypeStruct(shape, dtype)

    part_slab = slab // PARTS
    def pack(part):
        return pl.pallas_call(
            functools.partial(pack_kernel, col_devs),
            grid=(1,),
            out_shape=stacked((col_devs, CAP * part_slab + META, LANES)),
            in_specs=[pl.BlockSpec(memory_space=pltpu.HBM)] * 3 + [pl.BlockSpec((slots, feature, cells_sq // PARTS), lambda t: (0, 0, part))],
            out_specs=pl.BlockSpec((col_devs, CAP * part_slab + META, LANES), lambda t: (0, 0, 0)),
            scratch_shapes=[pltpu.SMEM((col_devs * CAP,), jnp.int32)]
            + [pltpu.SMEM((slots,), jnp.int32)] * 3
            + [pltpu.SemaphoreType.DMA((3,))],
            compiler_params=params(),
            cost_estimate=cost(3),
            name=f"pack_{part}",
        )(target, tile_square, tile_count, tiles_t)

    payloads = [lax.all_to_all(pack(0), "col", 0, 0, tiled=True), pack(1)]
    packed_cot = pl.pallas_call(
        pack_cotangent_kernel,
        out_shape=[stacked((cols // 2, bins, LANES))] * 2,
        in_specs=[SMEM, VMEM],
        out_specs=[VMEM] * 2,
        compiler_params=params(),
        cost_estimate=cost(2),
        name="pack_cotangent",
    )(where_am, cot_t)
    (*got_cot, over), land = mirror(*packed_cot)
    got_cot.append(land(over))
    payloads[1], *got_cot = lax.optimization_barrier((payloads[1], *got_cot))
    payloads[1] = lax.all_to_all(payloads[1], "col", 0, 0, tiled=True)

    turned = pl.pallas_call(
        turn_kernel,
        out_shape=stacked((entries, bins)),
        in_specs=[VMEM],
        out_specs=VMEM,
        scratch_shapes=[pltpu.VMEM((entries, LANES), F32)],
        compiler_params=params(),
        cost_estimate=cost(5),
        name="turn",
    )(cot_t)

    block = SQ // PARTS * cols
    steps = rows // SQ
    squares = entries // cells_sq
    whole = lambda *shape: pl.BlockSpec(shape, lambda t: (0,) * len(shape))
    blocks = 3 * hidden // width + 2
    sum_shape = (blocks // 2 * width, width)
    operands = (
        w_template,
        transition_norm_gain[None, :],
        transition_norm_bias[None, :],
        w_gate,
        w_up,
        w_out,
        w_gate.T,
        w_up.T,
        w_out.T,
        w_dist_t,
    )
    sums_shapes = [(width, 2 * hidden), (width, hidden), (feature + bins, width), (16, width)]
    part_heads = (cols // 2 // PARTS, bins, LANES)
    pair_cells = pair.reshape(entries, width)

    def transition(part, before):
        last = part == PARTS - 1
        per_step = lambda lanes: pl.BlockSpec((block, lanes), lambda t: (PARTS * t + part, 0))
        out_shape = [
            stacked((entries, width), F32),
            stacked((entries // PARTS, width)),
            stacked(part_heads),
            stacked(part_heads),
            stacked((col_devs, CAP * part_slab, LANES)),
        ]
        out_specs = [
            per_step(width),
            pl.BlockSpec((block, width), lambda t: (t, 0)),
            whole(*part_heads),
            whole(*part_heads),
            ANY,
        ]
        scratch = [
            pltpu.SMEM((col_devs * CAP,), jnp.int32),
            pltpu.VMEM((squares * part_slab, LANES), F32),
            pltpu.VMEM((squares * part_slab, LANES), BF16),
            pltpu.VMEM((squares, part_slab, LANES), BF16),
            pltpu.VMEM((block, 2 * hidden), BF16),
            pltpu.VMEM((block, hidden), BF16),
            pltpu.SemaphoreType.DMA((col_devs * CAP,)),
        ]
        if last:
            out_shape += [stacked(sum_shape, F32)] * 2
            out_specs += [whole(*sum_shape)] * 2
            scratch = [pltpu.VMEM(shape, F32) for shape in sums_shapes] + scratch
        else:
            out_shape += [stacked(shape, F32) for shape in sums_shapes]
            out_specs += [whole(*shape) for shape in sums_shapes]
        inputs = (where_am, payloads[part], pair_cells, turned, *got_cot, *operands)
        in_specs = [SMEM, whole(col_devs, CAP * part_slab + META, LANES), per_step(width), per_step(bins)]
        in_specs += [pl.BlockSpec((block // LANES, bins, LANES), lambda t: (t % (steps // 2) * PARTS + part, 0, 0))] * 3
        in_specs += [whole(*operand.shape) for operand in operands]
        aliases = {}
        if part:
            aliases = {len(inputs): 0}
            inputs += tuple(before)
            in_specs += [ANY] + [whole(*shape) for shape in sums_shapes]
        return pl.pallas_call(
            functools.partial(main_kernel, col_devs, cols, part),
            grid=(steps,),
            out_shape=out_shape,
            in_specs=in_specs,
            out_specs=out_specs,
            scratch_shapes=scratch,
            input_output_aliases=aliases,
            compiler_params=params(),
            cost_estimate=cost(20),
            name=f"transition_{part}",
        )(*inputs)

    before, z_low, got_heads, returned = None, [], [], []
    for part in range(PARTS):
        outs = transition(part, before)
        grad_pair = outs[0]
        before = (grad_pair, *outs[5:])
        z_low.append(outs[1])
        if part == PARTS - 1:
            keep, send = outs[5:]
            keep, send, returned[0], *got_heads[0] = lax.optimization_barrier((keep, send, *returned, *got_heads[0]))
            send = swap(send, "row", 1)
            got_heads[0][2] = land(got_heads[0][2])
        got, land = mirror(outs[2], outs[3])
        got_heads.append(got)
        returned.append(lax.all_to_all(outs[4], "col", 0, 0, tiled=True))

    heads = pl.pallas_call(
        heads_kernel,
        out_shape=stacked((cols, bins, rows)),
        in_specs=[VMEM] * (PARTS + 1),
        out_specs=VMEM,
        scratch_shapes=[pltpu.VMEM((entries, width), F32)],
        compiler_params=params(),
        cost_estimate=cost(5),
        name="own_heads",
    )(*z_low, w_dist_t)

    own = [heads]

    def heads_sent(value):
        got = lax.optimization_barrier((value, *got_heads[1], got_heads[0][2]))
        got_heads[0][2] = got[4]
        got_heads[1] = [got[1], got[2], land(got[3])]
        return got[0]

    def heads_landed(value):
        value, own[0], returned[1] = lax.optimization_barrier((value, own[0], returned[1]))
        return value

    if two_chips:
        pieces = all_sum_four(where_am, keep, send, (heads_sent, heads_landed))
    else:
        sums = all_sum(keep + send, (heads_sent, heads_landed))
        pieces = [jnp.concatenate([sums, swap(sums, "row", 1)])]
    def logits_of(part, before):
        half = SQ // PARTS
        there = pl.BlockSpec((half, bins, rows), lambda t: (PARTS * t + part, 0, 0))
        return pl.pallas_call(
            logits_kernel,
            grid=(cols // SQ,),
            out_shape=stacked((cols, bins, rows)),
            in_specs=[SMEM, there] + [pl.BlockSpec((half // 2, bins, LANES), lambda t: (t, 0, 0))] * 3 + [ANY] * part,
            out_specs=there,
            input_output_aliases={5: 0} if part else {},
            compiler_params=params(),
            cost_estimate=cost(2),
            name=f"logits_{part}",
        )(where_am, own[0], *got_heads[part], *before)

    def tile_gradients(part, before):
        return pl.pallas_call(
            functools.partial(tiles_kernel, col_devs),
            grid=(1,),
            out_shape=stacked((slots, feature, cells_sq)),
            in_specs=[SMEM] * 2 + [pl.BlockSpec((col_devs, CAP * part_slab, LANES), lambda t: (0, 0, 0))] + [ANY] * part,
            out_specs=pl.BlockSpec((slots, feature, cells_sq // PARTS), lambda t: (0, 0, part)),
            scratch_shapes=[pltpu.SMEM((col_devs * CAP,), jnp.int32)],
            input_output_aliases={3: 0} if part else {},
            compiler_params=params(),
            cost_estimate=cost(2),
            name=f"tile_gradients_{part}",
        )(target, tile_count, returned[part], *before)

    logits, grad_tiles = (), ()
    for part in range(PARTS):
        logits = (logits_of(part, logits),)
        grad_tiles = (tile_gradients(part, grad_tiles),)
    *pieces, logits, grad_tiles = lax.optimization_barrier((*pieces, logits[0], grad_tiles[0]))
    length = rows * row_devs
    weights = pl.pallas_call(
        functools.partial(weights_kernel, 1.0 / length),
        out_shape=[
            jax.ShapeDtypeStruct((feature, width), F32),
            jax.ShapeDtypeStruct((1, width), F32),
            jax.ShapeDtypeStruct((1, width), F32),
            jax.ShapeDtypeStruct((width, hidden), F32),
            jax.ShapeDtypeStruct((width, hidden), F32),
            jax.ShapeDtypeStruct((hidden, width), F32),
            jax.ShapeDtypeStruct((bins, width), F32),
        ],
        in_specs=[SMEM] + [VMEM] * len(pieces),
        out_specs=[VMEM] * 7,
        scratch_shapes=[pltpu.VMEM((2 * sum_shape[0], width), F32)],
        compiler_params=params(),
        cost_estimate=cost(2),
        name="weight_gradients",
    )(where_am, *pieces)
    g_template, g_gain, g_bias, g_gate, g_up, g_out, g_dist = weights
    return (
        jnp.transpose(logits, (2, 0, 1)),
        grad_pair.reshape(rows, cols, width),
        jnp.transpose(grad_tiles, (0, 2, 1)),
        g_template,
        g_gain[0],
        g_bias[0],
        g_gate,
        g_up,
        g_out,
        g_dist.T,
    )


def solution(mesh):
    split = P("row", "col", None)
    held = P(("row", "col"), None, None)
    return jax.shard_map(
        per_device,
        mesh=mesh,
        in_specs=(split, split, held, P(("row", "col"), None), P(("row", "col")), P(("row", "col")))
        + (P(),) * 7,
        out_specs=(split, split, held) + (P(),) * 7,
        check_vma=False,
    )
```

```python
import functools

import jax
import jax.numpy as jnp
from jax import lax
from jax.experimental import pallas as pl
from jax.experimental.pallas import tpu as pltpu
from jax.sharding import PartitionSpec as P

SQ = 32
CAP = 2
LANES = 128
META = 16
GROUP = LANES // SQ
PARTS = 2
PIECE = 256
VMEM_BYTES = 32 * 2**20
BF16 = jnp.bfloat16
F32 = jnp.float32

VMEM = pl.BlockSpec(memory_space=pltpu.VMEM)
SMEM = pl.BlockSpec(memory_space=pltpu.SMEM)
ANY = pl.BlockSpec(memory_space=pl.ANY)


def params():
    return pltpu.CompilerParams(vmem_limit_bytes=VMEM_BYTES)


def cost(micros):
    return pl.CostEstimate(flops=int(micros * 1.1e9), bytes_accessed=0, transcendentals=0)


def dot_nn(a, b):
    return lax.dot_general(a, b, (((1,), (0,)), ((), ())), preferred_element_type=F32)


def dot_nt(a, b):
    return lax.dot_general(a, b, (((1,), (1,)), ((), ())), preferred_element_type=F32)


def dot_tn(a, b):
    return lax.dot_general(a, b, (((0,), (0,)), ((), ())), preferred_element_type=F32)


def fill_slots(target, source, devs):
    def clear(i, unused):
        source[i] = -1
        return unused

    def place(s, unused):
        place_of = target[s] * CAP
        taken = source[place_of] >= 0
        source[place_of + jnp.where(taken, 1, 0)] = s
        return unused

    lax.fori_loop(0, devs * CAP, clear, 0)
    lax.fori_loop(0, target.shape[0], place, 0)


def low_lanes(shape):
    return lax.broadcasted_iota(jnp.int32, shape, 1) < LANES // 2


def pack_kernel(devs, target, square, count, tiles, payload, source, *scratch):
    *scalars, sems = scratch
    copies = [pltpu.make_async_copy(a, b, sems.at[i]) for i, (a, b) in enumerate(zip((target, square, count), scalars))]
    for copy in copies:
        copy.start()
    for copy in copies:
        copy.wait()
    target, square, count = scalars
    feature, cells = tiles.shape[1:]
    groups = cells // LANES
    fill_slots(target, source, devs)
    line = lax.broadcasted_iota(jnp.int32, (META, LANES), 0)
    for k in range(devs):
        meta = jnp.zeros((META, LANES), F32)
        for r in range(CAP):
            slot = source[k * CAP + r]
            held = jnp.maximum(slot, 0)
            ident = jnp.where(slot >= 0, square[held], -1).astype(F32)
            meta = jnp.where(line == r, ident, meta)
            meta = jnp.where(line == 8 + r, count[held].astype(F32), meta)
            for c in range(groups):
                at = (r * groups + c) * feature
                payload[k, at : at + feature, :] = tiles[held, :, c * LANES : (c + 1) * LANES]
        payload[k, CAP * groups * feature :, :] = meta.astype(BF16)


def pack_cotangent_kernel(where_am, cot, cot_a, cot_b):
    first = where_am[0] == 0
    low = low_lanes(cot.shape[1:])

    def pack_pair(p, unused):
        even, odd = cot[2 * p].astype(F32), cot[2 * p + 1].astype(F32)
        front = jnp.where(low, even, pltpu.roll(odd, LANES // 2, 1)).astype(BF16)
        back = jnp.where(low, pltpu.roll(even, LANES // 2, 1), odd).astype(BF16)
        cot_a[p] = jnp.where(first, front, back)
        cot_b[p] = jnp.where(first, back, front)
        return unused

    lax.fori_loop(0, cot.shape[0] // 2, pack_pair, 0, unroll=4)


def arrived(where_am, direct, routed, p):
    return jnp.where(where_am[2] != 0, routed[p].astype(F32), direct[p].astype(F32))


def turn_kernel(cot, out, turned):
    cols, bins, rows = cot.shape

    def turn(j, unused):
        turned[pl.ds(j, rows, stride=cols), 0:bins] = cot[j].astype(F32).T
        return unused

    lax.fori_loop(0, cols, turn, 0, unroll=4)
    out[...] = turned[:, 0:bins].astype(BF16)


def fold_rows(values):
    return jnp.sum(values.reshape(values.shape[0] // 8, 8, values.shape[1]), axis=0)


def share_out(where_am, sums, keep, send):
    acc_gu, acc_out, acc_td, acc_gb = sums
    width = acc_gu.shape[0]
    blocks = [acc_gu[:, c : c + width] for c in range(0, acc_gu.shape[1], width)]
    blocks += [acc_out[:, c : c + width] for c in range(0, acc_out.shape[1], width)]
    blocks += [acc_td[...], jnp.concatenate([acc_gb[...], jnp.zeros((width - 16, width), F32)], axis=0)]
    half = len(blocks) // 2
    for i in range(half):
        rows = slice(i * width, (i + 1) * width)

        @pl.when(where_am[1] == 0)
        def _():
            keep[rows, :] = blocks[i]
            send[rows, :] = blocks[half + i]

        @pl.when(where_am[1] != 0)
        def _():
            keep[rows, :] = blocks[half + i]
            send[rows, :] = blocks[i]


def main_kernel(devs, cols, part, *refs):
    (where_am, payloads), refs = refs[:2], refs[2:]
    (pair, turned, got_a, got_b, got_c), refs = refs[:5], refs[5:]
    (w_template, gain, bias, w_gate, w_up, w_out, w_gate_t, w_up_t, w_out_t, w_dist_t), refs = refs[:10], refs[10:]
    last = part == PARTS - 1
    if part:
        carried, refs = refs[1:5], refs[5:]
    (grad_pair, z_low_out, heads_a, heads_b, returns), refs = refs[:5], refs[5:]
    if last:
        (keep, send), refs = refs[:2], refs[2:]
    acc_gu, acc_out, acc_td, acc_gb = sums = refs[:4]
    idents, total, summed, squares, low_gu, low_hid, sems = refs[4:]
    step = pl.program_id(0)
    steps = pl.num_programs(0)
    feature, width = w_template.shape
    hidden = w_gate.shape[1]
    groups = SQ * SQ // LANES
    slab = groups // PARTS * feature
    block = pair.shape[0]
    rows = block // cols
    sq_cols = cols // SQ
    per_part = groups // PARTS

    @pl.when(step == 0)
    def _():
        total[...] = jnp.zeros_like(total)
        for i, acc in enumerate(sums):
            acc[...] = carried[i][...] if part else jnp.zeros_like(acc)
        metas = [payloads[k, CAP * slab :, :].astype(F32) for k in range(devs)]
        tops = [(k, r, jnp.max(metas[k][r : r + 1, :])) for k in range(devs) for r in range(CAP)]
        for k, r, top in tops:
            ident = top.astype(jnp.int32)
            idents[k * CAP + r] = ident
            scale = jnp.where(metas[k][r : r + 1, :] >= 0, 1.0 / metas[k][8 + r : 9 + r, :], 0.0)
            at = pl.multiple_of(jnp.maximum(ident, 0) * slab, slab)
            total[pl.ds(at, slab), :] += payloads[k, r * slab : (r + 1) * slab, :].astype(F32) * scale

        summed[...] = total[...].astype(BF16)

    proj, pieces = [], []
    for c in range(per_part):
        across = []
        for s in range(sq_cols):
            at = pl.multiple_of(((step * sq_cols + s) * per_part + c) * feature, feature)
            piece = summed[pl.ds(at, feature), :]
            across.append(dot_tn(piece, w_template[...]).reshape(GROUP, SQ, width))
            pieces.append(piece)
        proj.append(jnp.concatenate(across, axis=1).reshape(GROUP * cols, width))
    z_one = pair[...] + jnp.concatenate(proj, axis=0)
    mean = jnp.mean(z_one, axis=1, keepdims=True)
    centred = z_one - mean
    deviation = lax.rsqrt(jnp.mean(centred * centred, axis=1, keepdims=True) + 1e-5)
    standard = centred * deviation
    normed = (standard * gain[...] + bias[...]).astype(BF16)
    per_half = steps // 2
    pairs = block // LANES
    to = lax.rem(step, per_half) * pairs
    straight = step // per_half == where_am[0]
    mirrored = []
    for p in range(pairs):
        crossed = arrived(where_am, got_b, got_c, p)
        mirrored.append(jnp.where(straight, got_a[p].astype(F32), crossed).T)
    d_low = (turned[...].astype(F32) + jnp.concatenate(mirrored, axis=0)).astype(BF16)
    dz_two = dot_nn(d_low, w_dist_t[...])
    dz_low = dz_two.astype(BF16)

    z_two = z_one
    d_norm = jnp.zeros_like(z_one)
    for h in range(0, hidden, PIECE):
        e = h + PIECE
        gate = dot_nn(normed, w_gate[:, h:e])
        upper = dot_nn(normed, w_up[:, h:e])
        d_hidden = dot_nn(dz_low, w_out_t[:, h:e])
        sigma = 0.5 * jnp.tanh(0.5 * gate) + 0.5
        swish = gate * sigma
        hid = (swish * upper).astype(BF16)
        d_gate = (d_hidden * upper * (sigma + swish * (1.0 - sigma))).astype(BF16)
        d_upper = (d_hidden * swish).astype(BF16)
        z_two = z_two + dot_nn(hid, w_out[h:e, :])
        d_norm = d_norm + dot_nn(d_gate, w_gate_t[h:e, :]) + dot_nn(d_upper, w_up_t[h:e, :])
        low_hid[:, h:e] = hid
        low_gu[:, h:e] = d_gate
        low_gu[:, hidden + h : hidden + e] = d_upper

    acc_gu[...] += dot_tn(normed, low_gu[...])
    acc_out[...] += dot_tn(dz_low, low_hid[...])
    z_low = z_two.astype(BF16)
    z_low_out[...] = z_low
    acc_td[feature:, :] += dot_tn(d_low, z_low)
    acc_gb[0:8, :] += fold_rows(d_norm * standard)
    acc_gb[8:16, :] += fold_rows(d_norm)
    d_standard = d_norm * gain[...]
    grad = dz_two + deviation * (
        d_standard
        - jnp.mean(d_standard, axis=1, keepdims=True)
        - standard * jnp.mean(d_standard * standard, axis=1, keepdims=True)
    )
    grad_pair[...] = grad

    heads = dot_nt(w_dist_t[...], z_low).astype(BF16)

    @pl.when(straight)
    def _():
        for p in range(pairs):
            heads_a[to + p] = heads[:, p * LANES : (p + 1) * LANES]

    @pl.when(jnp.logical_not(straight))
    def _():
        for p in range(pairs):
            heads_b[to + p] = heads[:, p * LANES : (p + 1) * LANES]

    d_proj = grad.astype(BF16).reshape(rows, cols, width)
    for s in range(sq_cols):
        cells = d_proj[:, s * SQ : (s + 1) * SQ, :].reshape(rows * SQ, width)
        tile_grad = dot_nt(w_template[...], cells).astype(BF16)
        for c in range(per_part):
            squares[step * sq_cols + s, c * feature : (c + 1) * feature, :] = tile_grad[:, c * LANES : (c + 1) * LANES]
        side = jnp.concatenate([pieces[c * sq_cols + s] for c in range(per_part)], axis=1)
        acc_td[0:feature, :] += dot_nn(side, cells)

    @pl.when(step == steps - 1)
    def _():
        def copy_of(k, r):
            return pltpu.make_async_copy(
                squares.at[jnp.maximum(idents[k * CAP + r], 0)],
                returns.at[k, pl.ds(r * slab, slab)],
                sems.at[k * CAP + r],
            )

        for k in range(devs):
            for r in range(CAP):
                copy_of(k, r).start()
        if last:
            share_out(where_am, sums, keep, send)
        for k in range(devs):
            for r in range(CAP):
                copy_of(k, r).wait()


def heads_kernel(*refs):
    z_low, (w_dist_t, out, wide) = refs[:PARTS], refs[PARTS:]
    cols, bins, rows = out.shape
    block = SQ // PARTS * cols
    for part in range(PARTS):
        for band in range(rows // SQ):
            at = (band * PARTS + part) * block
            wide[at : at + block, :] = z_low[part][band * block : (band + 1) * block, :].astype(F32)

    def one(j, unused):
        column = wide[pl.ds(j, rows, stride=cols), :].astype(BF16)
        out[j] = dot_nt(w_dist_t[...], column).astype(BF16)
        return unused

    lax.fori_loop(0, cols, one, 0, unroll=8)


def logits_kernel(where_am, heads, got_a, got_b, got_c, *refs):
    out = refs[-1]
    straight = where_am[0] == 0
    low = low_lanes(heads.shape[1:])
    for p in range(got_a.shape[0]):
        a, b = got_a[p].astype(F32), arrived(where_am, got_b, got_c, p)
        front, back = jnp.where(straight, a, b), jnp.where(straight, b, a)
        even = jnp.where(low, front, pltpu.roll(back, LANES // 2, 1))
        odd = jnp.where(low, pltpu.roll(front, LANES // 2, 1), back)
        out[2 * p] = (heads[2 * p].astype(F32) + even).astype(BF16)
        out[2 * p + 1] = (heads[2 * p + 1].astype(F32) + odd).astype(BF16)


def tiles_kernel(devs, target, count, returned, *refs):
    out, source = refs[-2:]
    feature, cells = out.shape[1:]
    groups = cells // LANES
    fill_slots(target, source, devs)
    for k in range(devs):
        for r in range(CAP):
            slot = source[k * CAP + r]

            @pl.when(slot >= 0)
            def _():
                scale = 1.0 / jnp.full((1, LANES), count[slot].astype(F32), F32)
                for c in range(groups):
                    at = (r * groups + c) * feature
                    piece = returned[k, at : at + feature, :].astype(F32) * scale
                    out[slot, :, c * LANES : (c + 1) * LANES] = piece.astype(BF16)


def weights_kernel(scale, where_am, *refs):
    pieces, (g_template, g_gain, g_bias, g_gate, g_up, g_out, g_dist, total) = refs[:-8], refs[-8:]
    width, hidden = g_gate.shape
    feature = g_template.shape[0]
    per = hidden // width
    rows = pieces[0].shape[0] // 2
    half = rows * len(pieces)
    for m, piece in enumerate(pieces):
        for core in range(2):
            at = (where_am[1] ^ core) * half + (where_am[3] ^ m) * rows
            there = pl.ds(pl.multiple_of(at, 32), rows)
            total[there, :] = piece[core * rows : (core + 1) * rows, :].astype(F32) * scale

    def block(i):
        return total[i * width : (i + 1) * width, :]

    for c in range(per):
        at = slice(c * width, (c + 1) * width)
        g_gate[:, at] = block(c)
        g_up[:, at] = block(per + c)
        g_out[at, :] = block(2 * per + c).T
    both = block(3 * per)
    g_template[...] = both[:feature, :]
    g_dist[...] = both[feature:, :]
    last = block(3 * per + 1)
    g_gain[...] = jnp.sum(last[0:8, :], axis=0, keepdims=True)
    g_bias[...] = jnp.sum(last[8:16, :], axis=0, keepdims=True)


def axis_groups(axis, first, size):
    last = size.bit_length() - 1
    groups, bit = [], first
    while bit < last:
        wide = 1 if (last - bit) % 2 else 2
        groups.append((axis, bit, [m << bit for m in range(1, 1 << wide)]))
        bit += wide
    return groups


def swap(value, axis, mask):
    return lax.ppermute(value, axis, [(i, i ^ mask) for i in range(lax.axis_size(axis))])


def all_sum(value, settle):
    groups = axis_groups("row", 1, lax.axis_size("row")) + axis_groups("col", 0, lax.axis_size("col"))
    pairs = [(axis, bit) for axis, bit, masks in groups if len(masks) == 1]
    split = []
    for axis, bit in pairs:
        mine = (lax.axis_index(axis) >> bit) & 1
        both = value.reshape(2, value.shape[0] // 2, value.shape[1])
        away = lax.dynamic_index_in_dim(both, 1 - mine, 0, False).astype(BF16)
        value = lax.dynamic_index_in_dim(both, mine, 0, False) + swap(away, axis, 1 << bit).astype(F32)
        split.append(mine)
    value = settle[0](value)
    for axis, bit, masks in groups:
        if len(masks) == 1:
            continue
        low = value.astype(BF16)
        terms = [low.astype(F32)] + [swap(low, axis, m).astype(F32) for m in masks]
        while len(terms) > 1:
            terms = [terms[i] + terms[i + 1] for i in range(0, len(terms), 2)]
        value = terms[0]
    low = settle[1](value.astype(BF16))
    for (axis, bit), mine in reversed(list(zip(pairs, split))):
        other = swap(low, axis, 1 << bit)
        low = jnp.where(mine == 0, jnp.concatenate([low, other]), jnp.concatenate([other, low]))
    return low


def split_kernel(where_am, keep, got, mine, *sends):
    rows = mine.shape[0]
    for m, out in enumerate((mine, *sends)):
        at = pl.multiple_of((where_am[3] ^ m) * rows, 32)
        out[...] = (keep[pl.ds(at, rows), :] + got[pl.ds(at, rows), :]).astype(out.dtype)


def flip(value, m):
    rows, cols = lax.axis_size("row"), lax.axis_size("col")
    perm = [(r * cols + c, (r ^ (m & 2)) * cols + (c ^ (m & 1))) for r in range(rows) for c in range(cols)]
    return lax.ppermute(value, ("row", "col"), perm)


def all_sum_four(where_am, keep, got, settle):
    rows, width = keep.shape[0] // 4, keep.shape[1]
    mine, *sends = pl.pallas_call(
        split_kernel,
        out_shape=[jax.ShapeDtypeStruct((rows, width), F32 if m == 0 else BF16) for m in range(4)],
        in_specs=[SMEM] + [VMEM] * 2,
        out_specs=[VMEM] * 4,
        compiler_params=params(),
        cost_estimate=cost(1),
        name="split_sums",
    )(where_am, keep, got)
    a, b, c = [flip(send, m + 1).astype(F32) for m, send in enumerate(sends)]
    low = settle[0](((mine + a) + (b + c)).astype(BF16))
    a, b, c = [swap(low, "col", m).astype(F32) for m in (2, 4, 6)]
    low = settle[1](((low.astype(F32) + a) + (b + c)).astype(BF16))
    both = jnp.concatenate([low, swap(low, "row", 1)])
    return [both] + [flip(both, m) for m in (1, 2, 3)]


def per_device(
    pair,
    logit_cotangent,
    tiles,
    tile_target,
    tile_square,
    tile_count,
    w_template,
    transition_norm_gain,
    transition_norm_bias,
    w_gate,
    w_up,
    w_out,
    w_dist,
):
    row_devs = lax.axis_size("row")
    col_devs = lax.axis_size("col")
    rows, cols, width = pair.shape
    bins = w_dist.shape[1]
    hidden = w_gate.shape[1]
    slots, cells_sq, feature = tiles.shape
    groups = cells_sq // LANES
    slab = groups * feature
    entries = rows * cols
    halves = rows // cols
    my_row, my_col = lax.axis_index("row"), lax.axis_index("col")
    two_chips = row_devs == 4
    crosses = (my_col // halves // 2 != my_row // 2) & two_chips
    quarter = jnp.where(two_chips, my_row // 2 * 2 + my_col % 2, 0)
    where_am = jnp.stack([my_col % halves, my_row % 2, crosses.astype(jnp.int32), quarter]).astype(jnp.int32)
    target = tile_target[:, 0]
    tiles_t = jnp.transpose(tiles, (0, 2, 1))
    cot_t = jnp.transpose(logit_cotangent, (1, 2, 0))
    w_dist_t = w_dist.T

    def mirror(first, second):
        everywhere = [(r, c) for r in range(row_devs) for c in range(col_devs)]

        def move(value, steps):
            perm = [(a * col_devs + b, c * col_devs + d) for (a, b), (c, d) in steps]
            return lax.ppermute(value, ("row", "col"), perm)

        def ends(s):
            return [((r, c), (c // halves, halves * r + ((c % halves) ^ s))) for r, c in everywhere]

        direct = move(first, ends(0))
        if not two_chips:
            other = move(second, ends(1))
            return [direct, other, other], lambda value: value
        across = [((r, c), (e // 2 * 2 + r % 2, c), (e, f)) for (r, c), (e, f) in ends(1) if r // 2 != e // 2]
        stay = move(second, [(a, b) for a, b in ends(1) if a[0] // 2 == b[0] // 2])
        over = move(second, [(a, b) for a, b, c in across])
        return [direct, stay, over], lambda value: move(value, [(b, c) for a, b, c in across])

    def stacked(shape, dtype=BF16):
        return jax.ShapeDtypeStruct(shape, dtype)

    part_slab = slab // PARTS
    def pack(part):
        return pl.pallas_call(
            functools.partial(pack_kernel, col_devs),
            grid=(1,),
            out_shape=stacked((col_devs, CAP * part_slab + META, LANES)),
            in_specs=[pl.BlockSpec(memory_space=pltpu.HBM)] * 3 + [pl.BlockSpec((slots, feature, cells_sq // PARTS), lambda t: (0, 0, part))],
            out_specs=pl.BlockSpec((col_devs, CAP * part_slab + META, LANES), lambda t: (0, 0, 0)),
            scratch_shapes=[pltpu.SMEM((col_devs * CAP,), jnp.int32)]
            + [pltpu.SMEM((slots,), jnp.int32)] * 3
            + [pltpu.SemaphoreType.DMA((3,))],
            compiler_params=params(),
            cost_estimate=cost(3),
            name=f"pack_{part}",
        )(target, tile_square, tile_count, tiles_t)

    payloads = [lax.all_to_all(pack(0), "col", 0, 0, tiled=True), pack(1)]
    packed_cot = pl.pallas_call(
        pack_cotangent_kernel,
        out_shape=[stacked((cols // 2, bins, LANES))] * 2,
        in_specs=[SMEM, VMEM],
        out_specs=[VMEM] * 2,
        compiler_params=params(),
        cost_estimate=cost(2),
        name="pack_cotangent",
    )(where_am, cot_t)
    (*got_cot, over), land = mirror(*packed_cot)
    got_cot.append(land(over))
    payloads[1], *got_cot = lax.optimization_barrier((payloads[1], *got_cot))
    payloads[1] = lax.all_to_all(payloads[1], "col", 0, 0, tiled=True)

    turned = pl.pallas_call(
        turn_kernel,
        out_shape=stacked((entries, bins)),
        in_specs=[VMEM],
        out_specs=VMEM,
        scratch_shapes=[pltpu.VMEM((entries, LANES), F32)],
        compiler_params=params(),
        cost_estimate=cost(5),
        name="turn",
    )(cot_t)

    block = SQ // PARTS * cols
    steps = rows // SQ
    squares = entries // cells_sq
    whole = lambda *shape: pl.BlockSpec(shape, lambda t: (0,) * len(shape))
    blocks = 3 * hidden // width + 2
    sum_shape = (blocks // 2 * width, width)
    operands = (
        w_template,
        transition_norm_gain[None, :],
        transition_norm_bias[None, :],
        w_gate,
        w_up,
        w_out,
        w_gate.T,
        w_up.T,
        w_out.T,
        w_dist_t,
    )
    sums_shapes = [(width, 2 * hidden), (width, hidden), (feature + bins, width), (16, width)]
    part_heads = (cols // 2 // PARTS, bins, LANES)
    pair_cells = pair.reshape(entries, width)

    def transition(part, before):
        last = part == PARTS - 1
        per_step = lambda lanes: pl.BlockSpec((block, lanes), lambda t: (PARTS * t + part, 0))
        out_shape = [
            stacked((entries, width), F32),
            stacked((entries // PARTS, width)),
            stacked(part_heads),
            stacked(part_heads),
            stacked((col_devs, CAP * part_slab, LANES)),
        ]
        out_specs = [
            per_step(width),
            pl.BlockSpec((block, width), lambda t: (t, 0)),
            whole(*part_heads),
            whole(*part_heads),
            ANY,
        ]
        scratch = [
            pltpu.SMEM((col_devs * CAP,), jnp.int32),
            pltpu.VMEM((squares * part_slab, LANES), F32),
            pltpu.VMEM((squares * part_slab, LANES), BF16),
            pltpu.VMEM((squares, part_slab, LANES), BF16),
            pltpu.VMEM((block, 2 * hidden), BF16),
            pltpu.VMEM((block, hidden), BF16),
            pltpu.SemaphoreType.DMA((col_devs * CAP,)),
        ]
        if last:
            out_shape += [stacked(sum_shape, F32)] * 2
            out_specs += [whole(*sum_shape)] * 2
            scratch = [pltpu.VMEM(shape, F32) for shape in sums_shapes] + scratch
        else:
            out_shape += [stacked(shape, F32) for shape in sums_shapes]
            out_specs += [whole(*shape) for shape in sums_shapes]
        inputs = (where_am, payloads[part], pair_cells, turned, *got_cot, *operands)
        in_specs = [SMEM, whole(col_devs, CAP * part_slab + META, LANES), per_step(width), per_step(bins)]
        in_specs += [pl.BlockSpec((block // LANES, bins, LANES), lambda t: (t % (steps // 2) * PARTS + part, 0, 0))] * 3
        in_specs += [whole(*operand.shape) for operand in operands]
        aliases = {}
        if part:
            aliases = {len(inputs): 0}
            inputs += tuple(before)
            in_specs += [ANY] + [whole(*shape) for shape in sums_shapes]
        return pl.pallas_call(
            functools.partial(main_kernel, col_devs, cols, part),
            grid=(steps,),
            out_shape=out_shape,
            in_specs=in_specs,
            out_specs=out_specs,
            scratch_shapes=scratch,
            input_output_aliases=aliases,
            compiler_params=params(),
            cost_estimate=cost(20),
            name=f"transition_{part}",
        )(*inputs)

    before, z_low, got_heads, returned = None, [], [], []
    for part in range(PARTS):
        outs = transition(part, before)
        grad_pair = outs[0]
        before = (grad_pair, *outs[5:])
        z_low.append(outs[1])
        if part == PARTS - 1:
            keep, send = outs[5:]
            keep, send, returned[0], *got_heads[0] = lax.optimization_barrier((keep, send, *returned, *got_heads[0]))
            send = swap(send, "row", 1)
            got_heads[0][2] = land(got_heads[0][2])
        got, land = mirror(outs[2], outs[3])
        got_heads.append(got)
        returned.append(lax.all_to_all(outs[4], "col", 0, 0, tiled=True))

    heads = pl.pallas_call(
        heads_kernel,
        out_shape=stacked((cols, bins, rows)),
        in_specs=[VMEM] * (PARTS + 1),
        out_specs=VMEM,
        scratch_shapes=[pltpu.VMEM((entries, width), F32)],
        compiler_params=params(),
        cost_estimate=cost(5),
        name="own_heads",
    )(*z_low, w_dist_t)

    own = [heads]

    def heads_sent(value):
        got = lax.optimization_barrier((value, *got_heads[1], got_heads[0][2]))
        got_heads[0][2] = got[4]
        got_heads[1] = [got[1], got[2], land(got[3])]
        return got[0]

    def heads_landed(value):
        value, own[0], returned[1] = lax.optimization_barrier((value, own[0], returned[1]))
        return value

    if two_chips:
        pieces = all_sum_four(where_am, keep, send, (heads_sent, heads_landed))
    else:
        sums = all_sum(keep + send, (heads_sent, heads_landed))
        pieces = [jnp.concatenate([sums, swap(sums, "row", 1)])]
    def logits_of(part, before):
        half = SQ // PARTS
        there = pl.BlockSpec((half, bins, rows), lambda t: (PARTS * t + part, 0, 0))
        return pl.pallas_call(
            logits_kernel,
            grid=(cols // SQ,),
            out_shape=stacked((cols, bins, rows)),
            in_specs=[SMEM, there] + [pl.BlockSpec((half // 2, bins, LANES), lambda t: (t, 0, 0))] * 3 + [ANY] * part,
            out_specs=there,
            input_output_aliases={5: 0} if part else {},
            compiler_params=params(),
            cost_estimate=cost(2),
            name=f"logits_{part}",
        )(where_am, own[0], *got_heads[part], *before)

    def tile_gradients(part, before):
        return pl.pallas_call(
            functools.partial(tiles_kernel, col_devs),
            grid=(1,),
            out_shape=stacked((slots, feature, cells_sq)),
            in_specs=[SMEM] * 2 + [pl.BlockSpec((col_devs, CAP * part_slab, LANES), lambda t: (0, 0, 0))] + [ANY] * part,
            out_specs=pl.BlockSpec((slots, feature, cells_sq // PARTS), lambda t: (0, 0, part)),
            scratch_shapes=[pltpu.SMEM((col_devs * CAP,), jnp.int32)],
            input_output_aliases={3: 0} if part else {},
            compiler_params=params(),
            cost_estimate=cost(2),
            name=f"tile_gradients_{part}",
        )(target, tile_count, returned[part], *before)

    logits, grad_tiles = (), ()
    for part in range(PARTS):
        logits = (logits_of(part, logits),)
        grad_tiles = (tile_gradients(part, grad_tiles),)
    *pieces, logits, grad_tiles = lax.optimization_barrier((*pieces, logits[0], grad_tiles[0]))
    length = rows * row_devs
    weights = pl.pallas_call(
        functools.partial(weights_kernel, 1.0 / length),
        out_shape=[
            jax.ShapeDtypeStruct((feature, width), F32),
            jax.ShapeDtypeStruct((1, width), F32),
            jax.ShapeDtypeStruct((1, width), F32),
            jax.ShapeDtypeStruct((width, hidden), F32),
            jax.ShapeDtypeStruct((width, hidden), F32),
            jax.ShapeDtypeStruct((hidden, width), F32),
            jax.ShapeDtypeStruct((bins, width), F32),
        ],
        in_specs=[SMEM] + [VMEM] * len(pieces),
        out_specs=[VMEM] * 7,
        scratch_shapes=[pltpu.VMEM((2 * sum_shape[0], width), F32)],
        compiler_params=params(),
        cost_estimate=cost(2),
        name="weight_gradients",
    )(where_am, *pieces)
    g_template, g_gain, g_bias, g_gate, g_up, g_out, g_dist = weights
    return (
        jnp.transpose(logits, (2, 0, 1)),
        grad_pair.reshape(rows, cols, width),
        jnp.transpose(grad_tiles, (0, 2, 1)),
        g_template,
        g_gain[0],
        g_bias[0],
        g_gate,
        g_up,
        g_out,
        g_dist.T,
    )


def solution(mesh):
    split = P("row", "col", None)
    held = P(("row", "col"), None, None)
    return jax.shard_map(
        per_device,
        mesh=mesh,
        in_specs=(split, split, held, P(("row", "col"), None), P(("row", "col")), P(("row", "col")))
        + (P(),) * 7,
        out_specs=(split, split, held) + (P(),) * 7,
        check_vma=False,
    )
```
